128 devices in a mesh: az: 16 (over x_lo, z, core), rad: 8 (over y, x_hi).
Axes of the slice: x: 4 (x_hi: 2, x_lo: 2; x = x_hi * 2 + x_lo), y: 4, z: 4, core: 2. Of those that a mesh axis runs over, the one named last changes fastest.
Arguments:
- hidden_site_vector: bfloat16 [1, 256, 128, 512], P(None, 'az', 'rad')
- mesh_portion_descriptors: bfloat16 [262144, 128], P(('az', 'rad')), may hold values from -6 to 6
- mesh_entry_site: int32 [262144], P(('az', 'rad')), may hold values from 0 to 255
- mesh_portion_tally: int32 [128, 128], P(('az', 'rad')), may hold values from 0 to 16, as said below
- incline_grid_position: int32 [1], replicated, may hold values from 0 to 63
- incline_vector_lookup: bfloat16 [64, 512], replicated, may hold values from -6 to 6
- mesh_mapping_matrix: bfloat16 [128, 512], replicated, may hold values from -0.5 to 0.5
- prefocus_rescale_factor: float32 [2, 512], replicated, may hold values from 0.1 to 1.9
- probe_lock_payload_matrix: bfloat16 [2, 512, 1536], replicated, may hold values from -0.25 to 0.25
- sharpness_scale: float32 [2, 8], replicated, may hold values from 2 to 12
- final_mapping_matrix: bfloat16 [2, 512, 512], replicated, may hold values from -0.5 to 0.5
- terminal_rescale_factor: float32 [512], replicated, may hold values from 0.1 to 1.9
Outputs:
- latent: bfloat16 [1, 256, 128, 512], P(None, 'az', 'rad')
The draws below stay inside these ranges and needn't reach their ends.
Inputs may be any that keep to these rules, and one draw needn't show every extreme that they name: `mesh_portion_tally`: devices of radial index 0 (t % 8 == 0) get exactly 16 live rows from every source device; other blocks hold any number of live rows. `mesh_entry_site`: A cell local to the target device, numbered (plane * 16 + azimuth) * 16 + radius.
All inputs are finite; a program needn't handle non-finite values.
Results may differ from the reference program's by a relative error of at most 0.017.
Values may be sent and summed in bfloat16 or wider, within the bound.
No kernel may reach another device: no remote copies, remote signals or barrier semaphores. Data moves between devices by JAX's collectives and lax.ppermute only.
A program may use at most 64 MiB of HBM per device.

```python
import math
import jax
import jax.numpy as jnp
from jax import lax

HIDDEN_CHANNELS = 512
FOCUS_GROUPS = 8
CB = 128
PITCH = 64
HALO = 4
DEPTH_TOTAL = 2
AZ_DEV = 16
RAD_DEV = 16
PLANES = 1
SLOT = 16
HEAD_DIM = 64
PEERS = 128
BANDS = 8
NAZ = 256
NRAD = 128
CELLS_DEV = 256
SENDS = 2048
NODES = 262144


def draw_hidden_site_vector(key, part):
    key_scale, key_base = jax.random.split(key, 2)
    scale = jnp.exp(jax.random.uniform(key_scale, (PLANES, NAZ, NRAD, 1), jnp.float32, 0.0, math.log(8.0)))
    base = jax.random.normal(key_base, (PLANES, NAZ, NRAD, HIDDEN_CHANNELS), jnp.float32)
    return (base * scale).astype(jnp.bfloat16)


def draw_mesh_portion_tally(key, part):
    raw_counts = jax.random.randint(key, (PEERS, PEERS), 0, SLOT + 1, dtype=jnp.int32)
    target = jnp.arange(PEERS, dtype=jnp.int32)[None, :]
    return jnp.where(target % BANDS == 0, SLOT, raw_counts).astype(jnp.int32)


def place_ends(result, key, least, high):
    longest = result.shape.index(max(result.shape))
    spots = []
    for shift in (0, 1):
        where = [jax.random.randint(jax.random.fold_in(key, axis), (), 0, length) for axis, length in enumerate(result.shape)]
        where[longest] = (where[longest] + shift) % result.shape[longest]
        spots.append(tuple(where))
    return result.at[spots[0]].set(least).at[spots[1]].set(high)


def steps_of(rng, dims, shards, smallest, largest):
    level, own = 1.0, jax.random.fold_in(rng, 6)
    for dim, parts in shards:
        draws = jnp.exp(jax.random.uniform(jax.random.fold_in(own, dim), (parts,), jnp.float32, smallest / len(shards), largest / len(shards)))
        level = level * jnp.repeat(draws, dims[dim] // parts).reshape([-1 if axis == dim else 1 for axis in range(len(dims))])
    return level


def scatter_about(own_key, dims, deviation, most, shards=(), held_as=jnp.bfloat16):
    array = deviation * jax.random.normal(own_key, dims, jnp.float32)
    if shards:
        array = array * steps_of(own_key, dims, shards, -0.22, 0.18)
    return jnp.clip(array, -most, most).astype(held_as)


def setup_inputs(seed: int = 0) -> dict:
    seeds = jax.random.split(jax.random.key(seed), 13)
    hidden_site_vector = draw_hidden_site_vector(jax.random.fold_in(seeds[12], 71), 0)
    mesh_portion_descriptors = scatter_about(seeds[1], (NODES, CB), 1.0, 6.0, ((0, 128),))
    mesh_entry_site = place_ends(jax.random.randint(seeds[2], (NODES,), 0, CELLS_DEV), jax.random.fold_in(seeds[2], 1), 0, CELLS_DEV - 1).astype(jnp.int32)
    mesh_portion_tally = draw_mesh_portion_tally(jax.random.fold_in(seeds[12], 71), 0)
    incline_grid_position = jax.random.randint(seeds[4], (1,), 0, PITCH).astype(jnp.int32)
    incline_vector_lookup = scatter_about(seeds[5], (PITCH, HIDDEN_CHANNELS), 1.0, 6.0)
    mesh_mapping_matrix = scatter_about(seeds[6], (CB, HIDDEN_CHANNELS), CB ** -0.5, 0.5)
    prefocus_rescale_factor = jnp.clip(1.0 + 0.18 * jax.random.normal(seeds[7], (DEPTH_TOTAL, HIDDEN_CHANNELS), jnp.float32), 0.1, 1.9)
    probe_lock_payload_matrix = scatter_about(seeds[8], (DEPTH_TOTAL, HIDDEN_CHANNELS, 3 * HIDDEN_CHANNELS), HIDDEN_CHANNELS ** -0.5, 0.25)
    sharpness_scale = jnp.clip(jnp.exp(jax.random.uniform(seeds[9], (DEPTH_TOTAL, FOCUS_GROUPS), jnp.float32, math.log(2.0), math.log(12.0))), 2.0, 12.0)
    final_mapping_matrix = scatter_about(seeds[10], (DEPTH_TOTAL, HIDDEN_CHANNELS, HIDDEN_CHANNELS), (HIDDEN_CHANNELS // 4) ** -0.5, 0.5)
    terminal_rescale_factor = jnp.clip(1.0 + 0.18 * jax.random.normal(seeds[11], (HIDDEN_CHANNELS,), jnp.float32), 0.1, 1.9)
    return {"hidden_site_vector": hidden_site_vector, "mesh_portion_descriptors": mesh_portion_descriptors, "mesh_entry_site": mesh_entry_site, "mesh_portion_tally": mesh_portion_tally, "incline_grid_position": incline_grid_position, "incline_vector_lookup": incline_vector_lookup, "mesh_mapping_matrix": mesh_mapping_matrix, "prefocus_rescale_factor": prefocus_rescale_factor, "probe_lock_payload_matrix": probe_lock_payload_matrix, "sharpness_scale": sharpness_scale, "final_mapping_matrix": final_mapping_matrix, "terminal_rescale_factor": terminal_rescale_factor}


def rms_norm(matrix, gain):
    floats = matrix.astype(jnp.float32)
    return (floats * lax.rsqrt(lax.optimization_barrier(jnp.mean(floats * floats, -1, keepdims=True)) + 1e-05) * gain).astype(jnp.bfloat16)

def rescaled_groups(matrix, group_partitioned):
    floats = matrix.astype(jnp.float32)
    floats = floats.reshape(floats.shape[:-1] + (group_partitioned, floats.shape[-1] // group_partitioned))
    return floats * lax.rsqrt(lax.optimization_barrier(jnp.sum(floats * floats, -1, keepdims=True)) + 1e-06)

def window_attend(probe_direction, khat, value_heads, inside_window, reach_cells, rows_az, rows_rad):
    window = 2 * reach_cells + 1
    totals = jnp.zeros(probe_direction.shape[:-1], jnp.float32)
    for az_off in range(window):
        for rad_off in range(window):
            keys_here = khat[:, az_off:az_off + rows_az, rad_off:rad_off + rows_rad]
            scores = lax.optimization_barrier(jnp.sum(probe_direction * keys_here, -1))
            totals = totals + jnp.exp(scores) * inside_window[rad_off:rad_off + rows_rad][:, None]
    summed = jnp.zeros(probe_direction.shape, jnp.float32)
    for az_off in range(window):
        for rad_off in range(window):
            keys_here = khat[:, az_off:az_off + rows_az, rad_off:rad_off + rows_rad]
            scores = lax.optimization_barrier(jnp.sum(probe_direction * keys_here, -1))
            weight = (jnp.exp(scores) * inside_window[rad_off:rad_off + rows_rad][:, None] / totals).astype(jnp.bfloat16)
            values_here = value_heads[:, az_off:az_off + rows_az, rad_off:rad_off + rows_rad].astype(jnp.float32)
            summed = summed + weight.astype(jnp.float32)[..., None] * values_here
    return summed

def widen(matrix):
    looped = jnp.concatenate([matrix[:, -HALO:], matrix, matrix[:, :HALO]], axis=1)
    return jnp.pad(looped, ((0, 0), (0, 0), (HALO, HALO), (0, 0), (0, 0)))

def reference(hidden_site_vector, mesh_portion_descriptors, mesh_entry_site, mesh_portion_tally, incline_grid_position, incline_vector_lookup, mesh_mapping_matrix, prefocus_rescale_factor, probe_lock_payload_matrix, sharpness_scale, final_mapping_matrix, terminal_rescale_factor):
    node_index = jnp.arange(NODES, dtype=jnp.int32)
    source = node_index // SENDS
    target = node_index // SLOT % PEERS
    slot_pos = node_index % SLOT
    is_live = (slot_pos < mesh_portion_tally[source, target]).astype(jnp.float32)
    az_dev = target // BANDS
    rad_dev = target % BANDS
    plane_of = mesh_entry_site // (AZ_DEV * RAD_DEV)
    az_global = az_dev * AZ_DEV + mesh_entry_site // RAD_DEV % AZ_DEV
    rad_global = rad_dev * RAD_DEV + mesh_entry_site % RAD_DEV
    flat_cell = ((plane_of * NAZ + az_global) * NRAD + rad_global).astype(jnp.int32)
    features = mesh_portion_descriptors.astype(jnp.float32) * is_live[:, None]
    cell_sum = jax.ops.segment_sum(features, flat_cell, num_segments=PLANES * NAZ * NRAD)
    cell_feat = cell_sum.astype(jnp.bfloat16)
    encoded = jnp.dot(cell_feat, mesh_mapping_matrix, preferred_element_type=jnp.float32)
    pitch_row = incline_vector_lookup[incline_grid_position[0]].astype(jnp.float32)
    residual_state = (hidden_site_vector.reshape(-1, HIDDEN_CHANNELS).astype(jnp.float32) + encoded + pitch_row[None, :]).astype(jnp.bfloat16)
    residual_state = residual_state.reshape(PLANES, NAZ, NRAD, HIDDEN_CHANNELS)
    rad_pos = jnp.arange(NRAD + 2 * HALO, dtype=jnp.int32) - HALO
    inside_window = ((rad_pos >= 0) & (rad_pos < NRAD)).astype(jnp.float32)
    for depth_ordinal in range(DEPTH_TOTAL):
        normed = rms_norm(residual_state, prefocus_rescale_factor[depth_ordinal])
        mesh_descriptors_mapped = jnp.dot(normed.reshape(-1, HIDDEN_CHANNELS), probe_lock_payload_matrix[depth_ordinal], preferred_element_type=jnp.float32).astype(jnp.bfloat16)
        mesh_descriptors_mapped = mesh_descriptors_mapped.reshape(PLANES, NAZ, NRAD, 3 * HIDDEN_CHANNELS)
        probe_direction = rescaled_groups(mesh_descriptors_mapped[..., :HIDDEN_CHANNELS], FOCUS_GROUPS) * sharpness_scale[depth_ordinal][:, None]
        khat = widen(rescaled_groups(mesh_descriptors_mapped[..., HIDDEN_CHANNELS:2 * HIDDEN_CHANNELS], FOCUS_GROUPS))
        value_heads = widen(mesh_descriptors_mapped[..., 2 * HIDDEN_CHANNELS:].reshape(PLANES, NAZ, NRAD, FOCUS_GROUPS, HEAD_DIM))
        summed = window_attend(probe_direction, khat, value_heads, inside_window, HALO, NAZ, NRAD)
        attended = summed.reshape(-1, HIDDEN_CHANNELS).astype(jnp.bfloat16)
        update = jnp.dot(attended, final_mapping_matrix[depth_ordinal], preferred_element_type=jnp.float32)
        residual_state = (residual_state.reshape(-1, HIDDEN_CHANNELS).astype(jnp.float32) + update).astype(jnp.bfloat16).reshape(PLANES, NAZ, NRAD, HIDDEN_CHANNELS)
    return rms_norm(residual_state, terminal_rescale_factor)
```

```python
import functools

import jax
import jax.numpy as jnp
import numpy as np
from jax import lax
from jax.experimental import pallas as pl
from jax.experimental.pallas import tpu as pltpu
from jax.sharding import PartitionSpec as P

HALO = 4
HEADS = 8
WIDTH = 512
AZ = 16
RAD = 16
EDGE = 2 * HALO
NEG = -1024.0
LOG2E = 1.4426950408889634
COLUMN_J = np.array(
    list(range(8, 24)) + list(range(24, 28)) + list(range(4, 8)) + list(range(0, 4)) + list(range(28, 32))
)


def aug_tables():
    i = np.arange(32)
    key = np.zeros((32, 32, 64), np.float32)
    for d in range(24):
        key[:, :, d] = np.where(np.abs(COLUMN_J - COLUMN_J[d]) > HALO, NEG, 0.0)[None, :]
        key[:, :, 24 + d] = np.where(np.abs(i - (d + HALO)) > HALO, NEG, 0.0)[:, None]
    query = np.zeros((24, 24, 64), np.float32)
    for d in range(24):
        query[:, d, d] = 1.0
        query[d, :, 24 + d] = 1.0
    return np.concatenate([key, key], -1), np.concatenate([query, query], -1)


def norm_rows(x, gain):
    return x * lax.rsqrt(jnp.mean(x * x, -1, keepdims=True) + 1e-05) * gain


def dot(a, b):
    return jnp.dot(a, b, preferred_element_type=jnp.float32)


def rounded(x):
    return x.astype(jnp.bfloat16).astype(jnp.float32)


def cell_sum_kernel(arrived, feat, send_a, send_b):
    ids = jnp.sum(arrived[:, 16:24, :].astype(jnp.float32).reshape(16, 8, 8, 128), axis=1)
    cell = lax.broadcasted_iota(jnp.int32, (256, 128), 0).astype(jnp.float32)
    total = jnp.zeros((256, 128), jnp.float32)
    for step in range(8):
        picks = []
        for part in range(2):
            here = ids[2 * step + part]
            here = jnp.broadcast_to(here[None], (32, 8, 128)).reshape(256, 128)
            picks.append((here == cell).astype(jnp.float32).astype(jnp.bfloat16))
        rows = arrived[step * 16 : step * 16 + 16, 0:16, :].reshape(256, 128)
        total = total + dot(jnp.concatenate(picks, axis=1), rows)
    total = rounded(total).reshape(16, 16, 128)
    feat[...] = total.astype(jnp.bfloat16)
    even = lax.rem(lax.axis_index("rad"), 2) == 0
    low = total[:, :EDGE]
    high = total[:, EDGE:]
    send_a[...] = jnp.where(even, high, low).astype(jnp.bfloat16)
    send_b[...] = jnp.where(even, low, high).astype(jnp.bfloat16)


def cell_sums(arrived):
    edge = jax.ShapeDtypeStruct((16, EDGE, 128), jnp.bfloat16)
    return pl.pallas_call(
        cell_sum_kernel,
        out_shape=(jax.ShapeDtypeStruct((16, 16, 128), jnp.bfloat16), edge, edge),
        name="cell_sums",
    )(arrived)


def widen_kernel(own, got_a, got_b, full, send_a, send_b):
    channels = own.shape[-1]
    even_r = lax.rem(lax.axis_index("rad"), 2) == 0
    even_a = lax.rem(lax.axis_index("az"), 2) == 0
    first = lax.broadcasted_iota(jnp.int32, (16, EDGE, channels), 1) < HALO
    a = got_a[...].astype(jnp.float32)
    b = got_b[...].astype(jnp.float32)
    from_a = first == even_r
    near = jnp.where(from_a, a, b)
    far = jnp.where(from_a, b, a)
    wide = jnp.concatenate([own[...].astype(jnp.float32), near, far], axis=1)
    full[...] = wide.astype(jnp.bfloat16)
    low = wide[:EDGE]
    high = wide[EDGE:]
    send_a[...] = jnp.where(even_a, high, low).astype(jnp.bfloat16)
    send_b[...] = jnp.where(even_a, low, high).astype(jnp.bfloat16)


def widen(own, got_a, got_b):
    channels = own.shape[-1]
    edge = jax.ShapeDtypeStruct((EDGE, 32, channels), jnp.bfloat16)
    return pl.pallas_call(
        widen_kernel,
        out_shape=(jax.ShapeDtypeStruct((16, 32, channels), jnp.bfloat16), edge, edge),
        name="widen",
    )(own, got_a, got_b)


def layers_kernel(
    pitch_at,
    sharp,
    hid,
    hid_a,
    hid_b,
    feat,
    feat_a,
    feat_b,
    lookup,
    w_map,
    gains,
    w_qkv,
    w_out,
    last_gain,
    key_aug,
    query_aug,
    block_ones,
    out,
    kept,
    keys,
    values,
    queries,
    stream,
    att,
):
    even_a = lax.rem(lax.axis_index("az"), 2) == 0
    rows = lax.broadcasted_iota(jnp.int32, (64, 1), 0)
    pitch = jnp.sum(
        jnp.where(rows == pitch_at[0], lookup[...].astype(jnp.float32), 0.0), axis=0, keepdims=True
    )

    def low_half(shape):
        return lax.broadcasted_iota(jnp.int32, shape, len(shape) - 1) < 64

    def project(layer, block, normed, at, aug, target, scale=None):
        res = rounded(dot(normed, w_qkv[layer, :, block * 256 : block * 256 + 256]))
        size = res.shape[0]
        half = low_half((size, 128))
        if target is values:
            parts = res
            aug = jnp.ones((size, 128), jnp.float32)
        else:
            parts = res * lax.rsqrt(dot((res * res).astype(jnp.bfloat16), block_ones[...]) + 1e-06)
        for pair in range(2):
            tile = parts[:, pair * 128 : pair * 128 + 128]
            head = (block % 2) * 4 + pair * 2
            if scale is not None:
                tile = tile * jnp.where(half, scale[head], scale[head + 1])
            target[head, at : at + size] = jnp.where(half, tile, aug).astype(jnp.bfloat16)
            target[head + 1, at : at + size] = jnp.where(half, aug, tile).astype(jnp.bfloat16)

    def scales(layer):
        return [sharp[layer, head] * LOG2E for head in range(HEADS)]

    def attend(layer, at_query, n_query, at_key, n_key, before):
        half = low_half((n_query, 128))
        for pair in range(4):
            got = []
            for head in (2 * pair, 2 * pair + 1):
                score = lax.dot_general(
                    queries[head, pl.ds(at_query, n_query)],
                    keys[head, pl.ds(at_key, n_key)],
                    (((1,), (1,)), ((), ())),
                    preferred_element_type=jnp.float32,
                )
                got.append(dot(jnp.exp2(score).astype(jnp.bfloat16), values[head, pl.ds(at_key, n_key)]))
            top = jnp.where(half, got[0], got[1])
            bottom = pltpu.roll(jnp.where(half, got[1], got[0]), 64, 1)
            att[0:n_query, pair * 128 : pair * 128 + 128] = (top / bottom).astype(jnp.bfloat16)
        return rounded(before + dot(att[0:n_query], w_out[layer]))

    scale = scales(0)
    for chunk in range(4):
        if chunk == 0:
            h = jnp.where(even_a, hid_b[...].astype(jnp.float32), hid_a[...].astype(jnp.float32))
            f = jnp.where(even_a, feat_b[...].astype(jnp.float32), feat_a[...].astype(jnp.float32))
        elif chunk == 3:
            h = jnp.where(even_a, hid_a[...].astype(jnp.float32), hid_b[...].astype(jnp.float32))
            f = jnp.where(even_a, feat_a[...].astype(jnp.float32), feat_b[...].astype(jnp.float32))
        else:
            h = hid[8 * chunk - 8 : 8 * chunk].astype(jnp.float32)
            f = feat[8 * chunk - 8 : 8 * chunk].astype(jnp.float32)
        x = h.reshape(256, WIDTH) + dot(f.reshape(256, 128).astype(jnp.bfloat16), w_map[...])
        x = rounded(x + pitch)
        normed = norm_rows(x, gains[0:1, :])
        wide = normed.astype(jnp.bfloat16)
        aug = key_aug[8 * chunk : 8 * chunk + 8].astype(jnp.float32).reshape(256, 128)
        for block in (2, 3):
            project(0, block, wide, 256 * chunk, aug, keys)
        for block in (4, 5):
            project(0, block, wide, 256 * chunk, None, values)
        begin, end = (4, 8) if chunk == 0 else (0, 4) if chunk == 3 else (0, 8)
        count = (end - begin) * 24
        first = (8 * chunk + begin - 4) * 24
        kept[first : first + count] = (
            x.reshape(8, 32, WIDTH)[begin:end, :24].reshape(count, WIDTH).astype(jnp.bfloat16)
        )
        narrow = normed.reshape(8, 32, WIDTH)[begin:end, :24].reshape(count, WIDTH).astype(jnp.bfloat16)
        aug = query_aug[first : first + count].astype(jnp.float32)
        for block in (0, 1):
            project(0, block, narrow, first, aug, queries, scale)

    def group(g, carry):
        at = pl.multiple_of(g * 96, 96)
        x = attend(0, at, 96, pl.multiple_of(g * 128, 128), 384, kept[pl.ds(at, 96)].astype(jnp.float32))
        stream[pl.ds(at, 96)] = x.astype(jnp.bfloat16)
        return carry

    lax.fori_loop(0, 6, group, 0)

    scale = scales(1)
    for chunk in range(3):
        x = stream[192 * chunk : 192 * chunk + 192].astype(jnp.float32)
        normed = norm_rows(x, gains[1:2, :])
        wide = normed.astype(jnp.bfloat16)
        aug = key_aug[4 + 8 * chunk : 12 + 8 * chunk].astype(jnp.float32)[:, :24].reshape(192, 128)
        for block in (2, 3):
            project(1, block, wide, 192 * chunk, aug, keys)
        for block in (4, 5):
            project(1, block, wide, 192 * chunk, None, values)
        begin, end = (4, 8) if chunk == 0 else (0, 4) if chunk == 2 else (0, 8)
        count = (end - begin) * 16
        first = (8 * chunk + begin - 4) * 16
        kept[first : first + count] = (
            x.reshape(8, 24, WIDTH)[begin:end, :16].reshape(count, WIDTH).astype(jnp.bfloat16)
        )
        narrow = normed.reshape(8, 24, WIDTH)[begin:end, :16].reshape(count, WIDTH).astype(jnp.bfloat16)
        aug = query_aug[192 * chunk : 192 * chunk + 192].astype(jnp.float32).reshape(8, 24, 128)
        aug = aug[begin:end, :16].reshape(count, 128)
        for block in (0, 1):
            project(1, block, narrow, first, aug, queries, scale)
    for g in range(2):
        x = attend(1, 128 * g, 128, 192 * g, 384, kept[128 * g : 128 * g + 128].astype(jnp.float32))
        latent = norm_rows(x, last_gain[...])
        out[8 * g : 8 * g + 8] = latent.reshape(8, 16, WIDTH).astype(jnp.bfloat16)


def run_layers(pitch_at, sharp, *arrays):
    smem = pl.BlockSpec(memory_space=pltpu.SMEM)
    vmem = pl.BlockSpec(memory_space=pltpu.VMEM)
    return pl.pallas_call(
        layers_kernel,
        out_shape=jax.ShapeDtypeStruct((AZ, RAD, WIDTH), jnp.bfloat16),
        in_specs=[smem, smem] + [vmem] * len(arrays),
        out_specs=vmem,
        scratch_shapes=[
            pltpu.VMEM((576, WIDTH), jnp.bfloat16),
            pltpu.VMEM((HEADS, 1024, 128), jnp.bfloat16),
            pltpu.VMEM((HEADS, 1024, 128), jnp.bfloat16),
            pltpu.VMEM((HEADS, 576, 128), jnp.bfloat16),
            pltpu.VMEM((576, WIDTH), jnp.bfloat16),
            pltpu.VMEM((128, WIDTH), jnp.bfloat16),
        ],
        compiler_params=pltpu.CompilerParams(vmem_limit_bytes=48 << 20),
        name="layers",
    )(pitch_at, sharp, *arrays)


def swap(x, axis, shift):
    count = lax.axis_size(axis)
    pairs = [(i, ((i + shift) ^ 1) - shift) for i in range(count)]
    if axis == "az":
        pairs = [(i, j % count) for i, j in pairs]
    return lax.ppermute(x, axis, [(i, j) for i, j in pairs if 0 <= j < count])


def per_device(
    hidden_site_vector,
    mesh_portion_descriptors,
    mesh_entry_site,
    mesh_portion_tally,
    incline_grid_position,
    incline_vector_lookup,
    mesh_mapping_matrix,
    prefocus_rescale_factor,
    probe_lock_payload_matrix,
    sharpness_scale,
    final_mapping_matrix,
    terminal_rescale_factor,
):
    r = lax.axis_index("rad")
    even_r = lax.rem(r, 2) == 0

    slot = jnp.arange(16, dtype=jnp.int32)
    live = slot[None, :] < mesh_portion_tally[0][:, None]
    ids = jnp.where(live, mesh_entry_site.reshape(128, 16), 256).astype(jnp.bfloat16)
    ids = jnp.where(jnp.arange(128)[None, :] // 16 == r, jnp.tile(ids, (1, 8)), 0)
    packed = jnp.concatenate(
        [
            mesh_portion_descriptors.reshape(128, 16, 128),
            jnp.broadcast_to(ids[:, None, :], (128, 8, 128)),
        ],
        axis=1,
    )
    arrived = lax.all_to_all(packed, ("az", "rad"), split_axis=0, concat_axis=0, tiled=True)

    hidden = hidden_site_vector[0]
    low, high = hidden[:, :EDGE], hidden[:, EDGE:]
    hid_ra = swap(jnp.where(even_r, high, low), "rad", 0)
    hid_rb = swap(jnp.where(even_r, low, high), "rad", 1)
    hid, to_a, to_b = widen(hidden, hid_ra, hid_rb)
    hid_a = swap(to_a, "az", 0)
    hid_b = swap(to_b, "az", 1)

    feat, to_a, to_b = cell_sums(arrived)
    feat, to_a, to_b = widen(feat, swap(to_a, "rad", 0), swap(to_b, "rad", 1))
    feat_a = swap(to_a, "az", 0)
    feat_b = swap(to_b, "az", 1)

    key_aug, query_aug = aug_tables()
    m = r * RAD - EDGE + jnp.asarray(COLUMN_J, jnp.int32)
    outside = (m < 0) | (m >= RAD * lax.axis_size("rad"))
    rad_lane = np.arange(128) % 64 < 24
    key_aug = jnp.where(outside[None, :, None] & rad_lane[None, None, :], NEG, key_aug).astype(jnp.bfloat16)
    query_aug = jnp.asarray(query_aug.reshape(576, 128), jnp.bfloat16)
    block_ones = jnp.asarray(np.kron(np.eye(4), np.ones((64, 64))), jnp.bfloat16)
    out = run_layers(
        incline_grid_position,
        sharpness_scale,
        hid,
        hid_a,
        hid_b,
        feat,
        feat_a,
        feat_b,
        incline_vector_lookup,
        mesh_mapping_matrix,
        prefocus_rescale_factor,
        probe_lock_payload_matrix,
        final_mapping_matrix,
        terminal_rescale_factor[None, :],
        key_aug,
        query_aug,
        block_ones,
    )
    return out[None]


def solution(mesh):
    rows = P(("az", "rad"), None)
    in_specs = (P(None, "az", "rad", None), rows, P(("az", "rad")), rows) + (P(),) * 8
    return jax.shard_map(
        per_device,
        mesh=mesh,
        in_specs=in_specs,
        out_specs=P(None, "az", "rad", None),
        check_vma=False,
    )
```

```python
import jax
import jax.numpy as jnp
import numpy as np
from jax import lax
from jax.experimental import pallas as pl
from jax.experimental.pallas import tpu as pltpu
from jax.sharding import PartitionSpec as P

HALO = 4
HEADS = 8
WIDTH = 512
EDGE = 2 * HALO
DEAD = 256
NEG = -1024.0
LOG2E = 1.4426950408889634
COLUMN_J = np.array(
    list(range(8, 24)) + list(range(24, 28)) + list(range(4, 8)) + list(range(0, 4)) + list(range(28, 32))
)
SMEM = pl.BlockSpec(memory_space=pltpu.SMEM)
VMEM = pl.BlockSpec(memory_space=pltpu.VMEM)
HBM = pl.BlockSpec(memory_space=pltpu.HBM)


def window_tables():
    i = np.arange(32)
    key = np.zeros((32, 32, 128), np.float32)
    query = np.zeros((24, 24, 128), np.float32)
    for d in range(24):
        key[:, :, d] = np.where(np.abs(COLUMN_J - COLUMN_J[d]) > HALO, NEG, 0.0)[None, :]
        key[:, :, 24 + d] = np.where(np.abs(i - (d + HALO)) > HALO, NEG, 0.0)[:, None]
        query[:, d, d] = 1.0
        query[d, :, 24 + d] = 1.0
    key[:, :, 48] = np.where(COLUMN_J < 8, NEG, 0.0)[None, :]
    key[:, :, 49] = np.where(COLUMN_J >= 24, NEG, 0.0)[None, :]
    tables = (
        query.reshape(576, 128),
        key.reshape(1024, 128),
        query[4:20, :16].reshape(256, 128),
        key[4:28, :24].reshape(576, 128),
    )
    return [jnp.asarray(t, jnp.bfloat16) for t in tables]


def dot(a, b):
    return jnp.dot(a, b, preferred_element_type=jnp.float32)


def rounded(x):
    return x.astype(jnp.bfloat16).astype(jnp.float32)


def norm_rows(x, gain):
    return x * lax.rsqrt(jnp.mean(x * x, -1, keepdims=True) + 1e-05) * gain


def shape_of(x):
    return x if isinstance(x, jax.ShapeDtypeStruct) else jax.ShapeDtypeStruct(x, jnp.bfloat16)


COST = {"pack": 1.5, "stage": 3, "cell_sums": 2, "band": 1.5, "inner": 4, "outer": 8}


def call(kernel, name, outs, in_specs, out_specs=None, scratch=(), mib=8):
    return pl.pallas_call(
        kernel,
        out_shape=[shape_of(x) for x in outs],
        in_specs=in_specs,
        out_specs=out_specs or [VMEM] * len(outs),
        scratch_shapes=scratch,
        compiler_params=pltpu.CompilerParams(vmem_limit_bytes=mib << 20),
        name=name,
        cost_estimate=pl.CostEstimate(
            flops=int(COST[name] * 1e9), bytes_accessed=int(COST[name] * 3e6), transcendentals=0
        ),
    )


def interleave(tasks, depth):
    waiting = list(tasks)
    active = []
    while waiting or active:
        if waiting and len(active) < depth:
            active.append(waiting.pop(0))
        for task in list(active):
            if next(task, True):
                active.remove(task)


def one_by_one(*tasks):
    for task in tasks:
        yield from task


def pack_kernel(rows, cells, tally, packed, token, block, cells_here, tally_here, sems, out_sems):
    parts = [pl.ds(32 * i, 32) for i in range(4)]
    loads = [pltpu.make_async_copy(rows.at[at], block.at[at, 0:16, :], sems.at[i]) for i, at in enumerate(parts)]
    ids_load = pltpu.make_async_copy(cells, cells_here, sems.at[4])
    tally_load = pltpu.make_async_copy(tally, tally_here, sems.at[5])
    ids_load.start()
    tally_load.start()
    for load in loads:
        load.start()
    k = lax.broadcasted_iota(jnp.int32, (16, 128), 0)
    t = lax.broadcasted_iota(jnp.int32, (16, 128), 1)
    a = lax.broadcasted_iota(jnp.int32, (128, 128), 0)
    b = lax.broadcasted_iota(jnp.int32, (128, 128), 1)
    pick = jnp.where(lax.rem(a, 8) == b // 16, 1.0, 0.0).astype(jnp.bfloat16)
    r = lax.axis_index("rad")
    mine = t // 16 == r
    ids_load.wait()
    tally_load.wait()
    spread = jnp.where(t // 8 == k, tally_here[...].astype(jnp.float32), 0.0).astype(jnp.bfloat16)
    live = lax.rem(t, 16).astype(jnp.float32) < dot(spread, pick)
    ids = jnp.where(live, cells_here[...].astype(jnp.float32), float(DEAD))
    turned = [jnp.where(mine, pltpu.roll(ids, lax.rem(r - b + 8, 8) * 16, 1), 0.0) for b in range(8)]
    stores = []
    for i, at in enumerate(parts):
        for k in range(4 * i, 4 * i + 4):
            for b in range(8):
                row = jnp.broadcast_to(turned[b][k : k + 1], (8, 128))
                block[8 * k + b, 16:24, :] = row.astype(jnp.bfloat16)
        loads[i].wait()
        stores.append(pltpu.make_async_copy(block.at[at], packed.at[at], out_sems.at[i]))
        stores[-1].start()
    token[...] = jnp.zeros((8, 128), jnp.float32)
    for store in stores:
        store.wait()


def pack(rows, cells, tally):
    return call(
        pack_kernel,
        "pack",
        [(128, 24, 128), jax.ShapeDtypeStruct((8, 128), jnp.float32)],
        [HBM] * 3,
        [HBM, VMEM],
        [
            pltpu.VMEM((128, 24, 128), jnp.bfloat16),
            pltpu.VMEM((16, 128), jnp.int32),
            pltpu.VMEM((1, 128), jnp.int32),
            pltpu.SemaphoreType.DMA((6,)),
            pltpu.SemaphoreType.DMA((4,)),
        ],
        mib=60,
    )(rows, cells, tally)


def stage_kernel(token, pitch_at, sharp, lookup, hidden, *refs):
    count = (len(refs) - 5) // 2
    sources, copies = refs[:count], refs[count : 2 * count]
    pitch, scale, send_a, send_b, sems = refs[2 * count :]
    moves = [pltpu.make_async_copy(a, b, sems.at[i]) for i, (a, b) in enumerate(zip(sources, copies))]
    for move in moves:
        move.start()
    rows = lax.broadcasted_iota(jnp.int32, (64, 1), 0)
    pitch[...] = jnp.sum(
        jnp.where(rows == pitch_at[0], lookup[...].astype(jnp.float32), 0.0), axis=0, keepdims=True
    )
    head = lax.broadcasted_iota(jnp.int32, (1, WIDTH), 1) // 64
    for layer in range(2):
        line = token[0:1, 0:1] * jnp.ones((1, WIDTH), jnp.float32)
        for h in range(HEADS):
            line = jnp.where(head == h, sharp[layer, h] * LOG2E, line)
        scale[layer : layer + 1] = line
    even = lax.rem(lax.axis_index("rad"), 2) == 0
    low = hidden[:, :EDGE].astype(jnp.float32)
    high = hidden[:, EDGE:].astype(jnp.float32)
    send_a[...] = jnp.where(even, high, low).astype(jnp.bfloat16)
    send_b[...] = jnp.where(even, low, high).astype(jnp.bfloat16)
    for move in moves:
        move.wait()


def stage(token, pitch_at, sharp, lookup, hidden, *arrays):
    edge = (16, EDGE, WIDTH)
    row = jax.ShapeDtypeStruct((1, WIDTH), jnp.float32)
    two = jax.ShapeDtypeStruct((2, WIDTH), jnp.float32)
    return call(
        stage_kernel,
        "stage",
        [jax.ShapeDtypeStruct(x.shape, x.dtype) for x in arrays] + [row, two, edge, edge],
        [VMEM, SMEM, SMEM, VMEM, VMEM] + [HBM] * len(arrays),
        scratch=[pltpu.SemaphoreType.DMA((len(arrays),))],
        mib=24,
    )(token, pitch_at, sharp, lookup, hidden, *arrays)


def cell_sum_kernel(arrived, feat, send_a, send_b, block, sems):
    loads = [
        pltpu.make_async_copy(arrived.at[pl.ds(32 * i, 32)], block.at[pl.ds(32 * i, 32)], sems.at[i]) for i in range(4)
    ]
    for load in loads:
        load.start()
    cell = lax.broadcasted_iota(jnp.int32, (256, 128), 0).astype(jnp.float32)
    total = jnp.zeros((256, 128), jnp.float32)
    for step in range(4):
        loads[step].wait()
        here = slice(step * 32, step * 32 + 32)
        ids = jnp.sum(block[here, 16:24, :].astype(jnp.float32).reshape(4, 8, 8, 128), axis=1)
        picks = []
        for part in range(4):
            wide = jnp.broadcast_to(ids[part][None], (32, 8, 128)).reshape(256, 128)
            picks.append(jnp.where(wide == cell, 1.0, 0.0).astype(jnp.bfloat16))
        total = total + dot(jnp.concatenate(picks, axis=1), block[here, 0:16, :].reshape(512, 128))
    total = rounded(total).reshape(16, 16, 128)
    feat[...] = total.astype(jnp.bfloat16)
    even = lax.rem(lax.axis_index("rad"), 2) == 0
    low = total[:, :EDGE]
    high = total[:, EDGE:]
    send_a[...] = jnp.where(even, high, low).astype(jnp.bfloat16)
    send_b[...] = jnp.where(even, low, high).astype(jnp.bfloat16)


def cell_sums(arrived):
    return call(
        cell_sum_kernel,
        "cell_sums",
        [(16, 16, 128), (16, EDGE, 128), (16, EDGE, 128)],
        [HBM],
        scratch=[pltpu.VMEM((128, 24, 128), jnp.bfloat16), pltpu.SemaphoreType.DMA((4,))],
    )(arrived)


def band_kernel(feat, feat_a, feat_b, hid, hid_a, hid_b, pitch, w_map, first, second):
    even = lax.rem(lax.axis_index("rad"), 2) == 0

    def wide(own, got_a, got_b, at):
        here = slice(at, at + 8)
        a = got_a[here].astype(jnp.float32)
        b = got_b[here].astype(jnp.float32)
        from_a = (lax.broadcasted_iota(jnp.int32, a.shape, 1) < HALO) == even
        parts = [own[here].astype(jnp.float32), jnp.where(from_a, a, b), jnp.where(from_a, b, a)]
        return jnp.concatenate(parts, axis=1).reshape(256, a.shape[-1])

    for at, out in ((0, first), (8, second)):
        x = dot(wide(feat, feat_a, feat_b, at).astype(jnp.bfloat16), w_map[...])
        x = wide(hid, hid_a, hid_b, at) + x + pitch[...]
        out[...] = x.reshape(8, 32, WIDTH).astype(jnp.bfloat16)


def band(*arrays):
    return call(band_kernel, "band", [(EDGE, 32, WIDTH)] * 2, [VMEM] * 8)(*arrays)


def project(w, layer, block, rows, block_ones, target, at, scale=None, plain=False):
    x = dot(rows, w[layer, :, block * 256 : block * 256 + 256])
    lanes = slice(block % 2 * 256, block % 2 * 256 + 256)
    yield
    if not plain:
        x = rounded(x)
        squares = dot((x * x).astype(jnp.bfloat16), block_ones[...])
        yield
        x = x * lax.rsqrt(squares + 1e-06)
    if scale is not None:
        x = x * scale[layer : layer + 1, lanes]
    target[at : at + x.shape[0], lanes] = x.astype(jnp.bfloat16)


def project_all(w, layer, wide, narrow, block_ones, scale, queries, q_at, keys, values, at):
    parts = [project(w, layer, block, wide, block_ones, keys, at) for block in (2, 3)]
    parts += [project(w, layer, block, narrow, block_ones, queries, q_at, scale) for block in (0, 1)]
    return parts + [project(w, layer, block, wide, block_ones, values, at, plain=True) for block in (4, 5)]


def query_lanes(table):
    r = lax.axis_index("rad")
    lane = lax.broadcasted_iota(jnp.int32, (1, 128), 1)
    ends = ((lane == 48) & (r == 0)) | ((lane == 49) & (r == lax.axis_size("rad") - 1))
    return table + jnp.where(ends, 1.0, 0.0).astype(jnp.bfloat16)


def attend(queries, query_aug, keys, key_aug, values, att):
    n = query_aug.shape[0]
    lane = lax.broadcasted_iota(jnp.int32, (1, 128), 1)
    low = jnp.where(lane < 64, 1.0, 0.0).astype(jnp.bfloat16)
    high = jnp.where(lane < 64, 0.0, 1.0).astype(jnp.bfloat16)
    half = lax.broadcasted_iota(jnp.int32, (n, 128), 1) < 64
    one = jnp.ones((key_aug.shape[0], 128), jnp.bfloat16)

    def pair_of_heads(pair):
        lanes = slice(pair * 128, pair * 128 + 128)

        def rows(parts):
            return jnp.concatenate([ref[at : at + count, lanes] for ref, at, count in parts], axis=0)

        q = rows(queries)
        q = jnp.concatenate(
            [jnp.concatenate([q * low, query_aug], axis=1), jnp.concatenate([q * high, query_aug], axis=1)], axis=0
        )
        k = jnp.concatenate([rows(keys), key_aug], axis=1)
        score = lax.dot_general(q, k, (((1,), (1,)), ((), ())), preferred_element_type=jnp.float32)
        yield
        got = dot(jnp.exp2(score).astype(jnp.bfloat16), jnp.concatenate([rows(values), one], axis=1))
        yield
        top = jnp.where(half, got[:n, :128], got[n:, :128])
        total = jnp.where(half, got[:n, 128:], got[n:, 128:])
        att[0:n, lanes] = (top / total).astype(jnp.bfloat16)

    return [pair_of_heads(pair) for pair in range(HEADS // 2)]


def columns(x, at, count, width):
    return x[at : at + count, :width].reshape(count * width, WIDTH)


def inner_kernel(
    first, second, scale, gains, w_qkv, w_out, block_ones, q_aug, k_aug,
    queries, keys, values, stream, queries_1, keys_1, values_1, att,
):
    x = jnp.concatenate([first[...], second[...]], axis=0).astype(jnp.float32)
    normed = norm_rows(x.reshape(512, WIDTH), gains[0:1, :])
    narrow = columns(normed.reshape(16, 32, WIDTH), 0, 16, 24).astype(jnp.bfloat16)
    wide = normed.astype(jnp.bfloat16)
    interleave(project_all(w_qkv, 0, wide, narrow, block_ones, scale, queries, 0, keys, values, 0), 2)
    pairs = attend(
        [(queries, 96, 192)], query_lanes(q_aug[192:384]), [(keys, 0, 512)], k_aug[256:768], [(values, 0, 512)], att
    )
    interleave(pairs, 2)
    x = rounded(columns(x, 4, 8, 24) + dot(att[...], w_out[0]))
    stream[...] = x.astype(jnp.bfloat16)
    normed = norm_rows(x, gains[1:2, :])
    narrow = columns(normed.reshape(8, 24, WIDTH), 0, 8, 16).astype(jnp.bfloat16)
    wide = normed.astype(jnp.bfloat16)
    interleave(project_all(w_qkv, 1, wide, narrow, block_ones, scale, queries_1, 0, keys_1, values_1, 0), 2)


def inner(*arrays):
    outs = [(384, WIDTH), (512, WIDTH), (512, WIDTH), (192, WIDTH), (128, WIDTH), (192, WIDTH), (192, WIDTH)]
    scratch = [pltpu.VMEM((192, WIDTH), jnp.bfloat16)]
    return call(inner_kernel, "inner", outs, [VMEM] * 9, scratch=scratch, mib=14)(*arrays)


def outer_kernel(
    low, high, first, second, scale, gains, w_qkv, w_out, last_gain, block_ones, q_aug, k_aug, q_aug_1, k_aug_1,
    q_mid, k_mid, v_mid, stream_mid, q1_mid, k1_mid, v1_mid,
    out, q_end, k_end, v_end, q1_end, k1_end, v1_end, att_0, att_1,
):
    att = (att_0, att_1)
    x = jnp.concatenate([low[...], high[...]], axis=0).astype(jnp.float32)
    normed = norm_rows(x.reshape(512, WIDTH), gains[0:1, :])
    narrow = columns(normed.reshape(16, 32, WIDTH), 4, 8, 24).astype(jnp.bfloat16)
    wide = normed.astype(jnp.bfloat16)
    interleave(project_all(w_qkv, 0, wide, narrow, block_ones, scale, q_end, 0, k_end, v_end, 0), 2)
    pairs = []
    for part in range(2):
        if part == 0:
            q = [(q_end, 0, 96), (q_mid, 0, 96)]
            k, v = [[(end, 0, 256), (mid, 0, 256)] for end, mid in ((k_end, k_mid), (v_end, v_mid))]
        else:
            q = [(q_mid, 288, 96), (q_end, 96, 96)]
            k, v = [[(mid, 256, 256), (end, 256, 256)] for end, mid in ((k_end, k_mid), (v_end, v_mid))]
        q_lanes = query_lanes(q_aug[384 * part : 384 * part + 192])
        pairs.append(attend(q, q_lanes, k, k_aug[512 * part : 512 * part + 512], v, att[part]))
    kept = [None, None]

    def finish(part):
        at = 4 * (1 - part)
        ours = first if part == 0 else second
        before = [columns(x, 4 + 4 * part, 4, 24), columns(ours[...].astype(jnp.float32), 4 * part, 4, 24)]
        y = dot(att[part][...], w_out[0])
        yield
        y = rounded(jnp.concatenate(before if part == 0 else before[::-1], axis=0) + y)
        normed = norm_rows(y, gains[1:2, :])
        narrow = columns(normed.reshape(8, 24, WIDTH), at, 4, 16).astype(jnp.bfloat16)
        kept[part] = columns(y.reshape(8, 24, WIDTH), at, 4, 16)
        yield
        wide = normed.astype(jnp.bfloat16)
        yield from one_by_one(
            *project_all(
                w_qkv, 1, wide, narrow, block_ones, scale, q1_end, 64 * part, k1_end, v1_end, 192 * part
            )
        )

    interleave(pairs[0], 2)
    interleave([one_by_one(*pairs[1]), finish(0)], 2)
    middle = stream_mid[...].astype(jnp.float32).reshape(8, 24, WIDTH)
    pairs = []
    for part in range(2):
        if part == 0:
            q = [(q1_end, 0, 64), (q1_mid, 0, 64)]
            k, v = [[(end, 0, 192), (mid, 0, 192)] for end, mid in ((k1_end, k1_mid), (v1_end, v1_mid))]
        else:
            q = [(q1_mid, 64, 64), (q1_end, 64, 64)]
            k, v = [[(mid, 0, 192), (end, 192, 192)] for end, mid in ((k1_end, k1_mid), (v1_end, v1_mid))]
        q_lanes = query_lanes(q_aug_1[128 * part : 128 * part + 128])
        pairs.append(attend(q, q_lanes, k, k_aug_1[192 * part : 192 * part + 384], v, att[part]))

    def end(part):
        before = [columns(middle, 4 * part, 4, 16), kept[part]]
        y = dot(att[part][0:128], w_out[1])
        yield
        y = rounded(jnp.concatenate(before if part else before[::-1], axis=0) + y)
        latent = norm_rows(y, last_gain[...])
        out[8 * part : 8 * part + 8] = latent.reshape(8, 16, WIDTH).astype(jnp.bfloat16)

    interleave([finish(1), one_by_one(*pairs[0])], 2)
    interleave([one_by_one(*pairs[1]), end(0)], 2)
    interleave([end(1)], 1)


def outer(*arrays):
    scratch = [192, 512, 512, 128, 384, 384, 192, 192]
    return call(
        outer_kernel,
        "outer",
        [(16, 16, WIDTH)],
        [VMEM] * 21,
        scratch=[pltpu.VMEM((rows, WIDTH), jnp.bfloat16) for rows in scratch],
        mib=14,
    )(*arrays)[0]


def swap(x, shift):
    count = lax.axis_size("rad")
    pairs = [(i, ((i + shift) ^ 1) - shift) for i in range(count)]
    return lax.ppermute(x, "rad", [(i, j) for i, j in pairs if 0 <= j < count])


def pass_on(x, step):
    count = lax.axis_size("az")
    return lax.ppermute(x, "az", [(i, (i + step) % count) for i in range(count)])


def per_device(
    hidden_site_vector,
    mesh_portion_descriptors,
    mesh_entry_site,
    mesh_portion_tally,
    incline_grid_position,
    incline_vector_lookup,
    mesh_mapping_matrix,
    prefocus_rescale_factor,
    probe_lock_payload_matrix,
    sharpness_scale,
    final_mapping_matrix,
    terminal_rescale_factor,
):
    packed, token = pack(
        mesh_portion_descriptors.reshape(128, 16, 128), mesh_entry_site.reshape(16, 128), mesh_portion_tally
    )
    arrived = lax.all_to_all(packed, ("az", "rad"), split_axis=0, concat_axis=0, tiled=True)

    hidden = hidden_site_vector[0]
    block_ones = jnp.asarray(np.kron(np.eye(4), np.ones((64, 64))), jnp.bfloat16)
    gains, w_qkv, w_out, w_map, last_gain, block_ones, q_aug, k_aug, q_aug_1, k_aug_1, pitch, scale, to_a, to_b = stage(
        token,
        incline_grid_position,
        sharpness_scale,
        incline_vector_lookup,
        hidden,
        prefocus_rescale_factor,
        probe_lock_payload_matrix,
        final_mapping_matrix,
        mesh_mapping_matrix,
        terminal_rescale_factor[None, :],
        block_ones,
        *window_tables(),
    )
    hid_a, hid_b = swap(to_a, 0), swap(to_b, 1)

    feat, to_a, to_b = cell_sums(arrived)
    feat_a, feat_b = swap(to_a, 0), swap(to_b, 1)
    first, second = band(feat, feat_a, feat_b, hidden, hid_a, hid_b, pitch, w_map)
    low, high = pass_on(second, 1), pass_on(first, -1)
    middle = inner(first, second, scale, gains, w_qkv, w_out, block_ones, q_aug, k_aug)
    out = outer(
        low, high, first, second, scale, gains, w_qkv, w_out, last_gain,
        block_ones, q_aug, k_aug, q_aug_1, k_aug_1, *middle,
    )
    return out[None]


def solution(mesh):
    rows = P(("az", "rad"), None)
    in_specs = (P(None, "az", "rad", None), rows, P(("az", "rad")), rows) + (P(),) * 8
    return jax.shard_map(
        per_device,
        mesh=mesh,
        in_specs=in_specs,
        out_specs=P(None, "az", "rad", None),
        check_vma=False,
    )
```

```python
import jax
import jax.numpy as jnp
import numpy as np
from jax import lax
from jax.experimental import pallas as pl
from jax.experimental.pallas import tpu as pltpu
from jax.sharding import PartitionSpec as P

HALO = 4
HEADS = 8
WIDTH = 512
EDGE = 2 * HALO
DEAD = 256
NEG = -1024.0
LOG2E = 1.4426950408889634
COLUMN_J = np.array(
    list(range(8, 24)) + list(range(24, 28)) + list(range(4, 8)) + list(range(0, 4)) + list(range(28, 32))
)
SMEM = pl.BlockSpec(memory_space=pltpu.SMEM)
VMEM = pl.BlockSpec(memory_space=pltpu.VMEM)
HBM = pl.BlockSpec(memory_space=pltpu.HBM)


def window_tables():
    i = np.arange(32)
    key = np.zeros((32, 32, 128), np.float32)
    query = np.zeros((24, 24, 128), np.float32)
    for d in range(24):
        key[:, :, d] = np.where(np.abs(COLUMN_J - COLUMN_J[d]) > HALO, NEG, 0.0)[None, :]
        key[:, :, 24 + d] = np.where(np.abs(i - (d + HALO)) > HALO, NEG, 0.0)[:, None]
        query[:, d, d] = 1.0
        query[d, :, 24 + d] = 1.0
    key[:, :, 48] = np.where(COLUMN_J < 8, NEG, 0.0)[None, :]
    key[:, :, 49] = np.where(COLUMN_J >= 24, NEG, 0.0)[None, :]
    tables = (
        query.reshape(576, 128),
        key.reshape(1024, 128),
        query[4:20, :16].reshape(256, 128),
        key[4:28, :24].reshape(576, 128),
    )
    return [jnp.asarray(t, jnp.bfloat16) for t in tables]


def dot(a, b):
    return jnp.dot(a, b, preferred_element_type=jnp.float32)


def rounded(x):
    return x.astype(jnp.bfloat16).astype(jnp.float32)


def norm_rows(x, gain):
    return x * lax.rsqrt(jnp.mean(x * x, -1, keepdims=True) + 1e-05) * gain


def shape_of(x):
    return x if isinstance(x, jax.ShapeDtypeStruct) else jax.ShapeDtypeStruct(x, jnp.bfloat16)


COST = {"pack": 1.5, "stage": 1, "cell_sums": 2, "band": 1.5, "inner": 4, "outer": 8}


def call(kernel, name, outs, in_specs, out_specs=None, scratch=(), mib=8):
    return pl.pallas_call(
        kernel,
        out_shape=[shape_of(x) for x in outs],
        in_specs=in_specs,
        out_specs=out_specs or [VMEM] * len(outs),
        scratch_shapes=scratch,
        compiler_params=pltpu.CompilerParams(vmem_limit_bytes=mib << 20),
        name=name,
        cost_estimate=pl.CostEstimate(
            flops=int(COST[name] * 1e9), bytes_accessed=int(COST[name] * 3e6), transcendentals=0
        ),
    )


def interleave(tasks, depth):
    waiting = list(tasks)
    active = []
    while waiting or active:
        if waiting and len(active) < depth:
            active.append(waiting.pop(0))
        for task in list(active):
            if next(task, True):
                active.remove(task)


def one_by_one(*tasks):
    for task in tasks:
        yield from task


def pack_kernel(rows, cells, tally, packed, token, block, cells_here, tally_here, sems, out_sems):
    parts = [pl.ds(32 * i, 32) for i in range(4)]
    loads = [pltpu.make_async_copy(rows.at[at], block.at[at, 0:16, :], sems.at[i]) for i, at in enumerate(parts)]
    ids_load = pltpu.make_async_copy(cells, cells_here, sems.at[4])
    tally_load = pltpu.make_async_copy(tally, tally_here, sems.at[5])
    ids_load.start()
    tally_load.start()
    for load in loads:
        load.start()
    k = lax.broadcasted_iota(jnp.int32, (16, 128), 0)
    t = lax.broadcasted_iota(jnp.int32, (16, 128), 1)
    a = lax.broadcasted_iota(jnp.int32, (128, 128), 0)
    b = lax.broadcasted_iota(jnp.int32, (128, 128), 1)
    pick = jnp.where(lax.rem(a, 8) == b // 16, 1.0, 0.0).astype(jnp.bfloat16)
    r = lax.axis_index("rad")
    mine = t // 16 == r
    ids_load.wait()
    tally_load.wait()
    spread = jnp.where(t // 8 == k, tally_here[...].astype(jnp.float32), 0.0).astype(jnp.bfloat16)
    live = lax.rem(t, 16).astype(jnp.float32) < dot(spread, pick)
    ids = jnp.where(live, cells_here[...].astype(jnp.float32), float(DEAD))
    turned = [jnp.where(mine, pltpu.roll(ids, lax.rem(r - b + 8, 8) * 16, 1), 0.0) for b in range(8)]
    stores = []
    for i, at in enumerate(parts):
        for k in range(4 * i, 4 * i + 4):
            for b in range(8):
                row = jnp.broadcast_to(turned[b][k : k + 1], (8, 128))
                block[8 * k + b, 16:24, :] = row.astype(jnp.bfloat16)
        loads[i].wait()
        stores.append(pltpu.make_async_copy(block.at[at], packed.at[at], out_sems.at[i]))
        stores[-1].start()
    token[...] = jnp.zeros((8, 128), jnp.float32)
    for store in stores:
        store.wait()


def pack(rows, cells, tally):
    return call(
        pack_kernel,
        "pack",
        [(128, 24, 128), jax.ShapeDtypeStruct((8, 128), jnp.float32)],
        [HBM] * 3,
        [HBM, VMEM],
        [
            pltpu.VMEM((128, 24, 128), jnp.bfloat16),
            pltpu.VMEM((16, 128), jnp.int32),
            pltpu.VMEM((1, 128), jnp.int32),
            pltpu.SemaphoreType.DMA((6,)),
            pltpu.SemaphoreType.DMA((4,)),
        ],
        mib=60,
    )(rows, cells, tally)


def stage_kernel(token, pitch_at, sharp, lookup, hidden, pitch, scale, send_a, send_b):
    rows = lax.broadcasted_iota(jnp.int32, (64, 1), 0)
    pitch[...] = jnp.sum(
        jnp.where(rows == pitch_at[0], lookup[...].astype(jnp.float32), 0.0), axis=0, keepdims=True
    )
    head = lax.broadcasted_iota(jnp.int32, (1, WIDTH), 1) // 64
    for layer in range(2):
        line = token[0:1, 0:1] * jnp.ones((1, WIDTH), jnp.float32)
        for h in range(HEADS):
            line = jnp.where(head == h, sharp[layer, h] * LOG2E, line)
        scale[layer : layer + 1] = line
    even = lax.rem(lax.axis_index("rad"), 2) == 0
    low = hidden[:, :EDGE].astype(jnp.float32)
    high = hidden[:, EDGE:].astype(jnp.float32)
    send_a[...] = jnp.where(even, high, low).astype(jnp.bfloat16)
    send_b[...] = jnp.where(even, low, high).astype(jnp.bfloat16)


def stage(*arrays):
    edge = (16, EDGE, WIDTH)
    row = jax.ShapeDtypeStruct((1, WIDTH), jnp.float32)
    two = jax.ShapeDtypeStruct((2, WIDTH), jnp.float32)
    return call(stage_kernel, "stage", [row, two, edge, edge], [VMEM, SMEM, SMEM, VMEM, VMEM])(*arrays)


def cell_sum_kernel(block, feat, send_a, send_b):
    cell = lax.broadcasted_iota(jnp.int32, (256, 128), 0).astype(jnp.float32)
    total = jnp.zeros((256, 128), jnp.float32)
    for step in range(4):
        here = slice(step * 32, step * 32 + 32)
        ids = jnp.sum(block[here, 16:24, :].astype(jnp.float32).reshape(4, 8, 8, 128), axis=1)
        picks = []
        for part in range(4):
            wide = jnp.broadcast_to(ids[part][None], (32, 8, 128)).reshape(256, 128)
            picks.append(jnp.where(wide == cell, 1.0, 0.0).astype(jnp.bfloat16))
        total = total + dot(jnp.concatenate(picks, axis=1), block[here, 0:16, :].reshape(512, 128))
    total = rounded(total).reshape(16, 16, 128)
    feat[...] = total.astype(jnp.bfloat16)
    even = lax.rem(lax.axis_index("rad"), 2) == 0
    low = total[:, :EDGE]
    high = total[:, EDGE:]
    send_a[...] = jnp.where(even, high, low).astype(jnp.bfloat16)
    send_b[...] = jnp.where(even, low, high).astype(jnp.bfloat16)


def cell_sums(arrived):
    return call(
        cell_sum_kernel,
        "cell_sums",
        [(16, 16, 128), (16, EDGE, 128), (16, EDGE, 128)],
        [VMEM],
    )(arrived)


def band_kernel(feat, feat_a, feat_b, hid, hid_a, hid_b, pitch, w_map, first, second):
    even = lax.rem(lax.axis_index("rad"), 2) == 0

    def wide(own, got_a, got_b, at):
        here = slice(at, at + 8)
        a = got_a[here].astype(jnp.float32)
        b = got_b[here].astype(jnp.float32)
        from_a = (lax.broadcasted_iota(jnp.int32, a.shape, 1) < HALO) == even
        parts = [own[here].astype(jnp.float32), jnp.where(from_a, a, b), jnp.where(from_a, b, a)]
        return jnp.concatenate(parts, axis=1).reshape(256, a.shape[-1])

    for at, out in ((0, first), (8, second)):
        x = dot(wide(feat, feat_a, feat_b, at).astype(jnp.bfloat16), w_map[...])
        x = wide(hid, hid_a, hid_b, at) + x + pitch[...]
        out[...] = x.reshape(8, 32, WIDTH).astype(jnp.bfloat16)


def band(*arrays):
    return call(band_kernel, "band", [(EDGE, 32, WIDTH)] * 2, [VMEM] * 8)(*arrays)


def project(w, layer, block, rows, block_ones, target, at, scale=None, plain=False):
    x = dot(rows, w[layer, :, block * 256 : block * 256 + 256])
    lanes = slice(block % 2 * 256, block % 2 * 256 + 256)
    yield
    if not plain:
        x = rounded(x)
        squares = dot((x * x).astype(jnp.bfloat16), block_ones[...])
        yield
        x = x * lax.rsqrt(squares + 1e-06)
    if scale is not None:
        x = x * scale[layer : layer + 1, lanes]
    target[at : at + x.shape[0], lanes] = x.astype(jnp.bfloat16)


def project_all(w, layer, wide, narrow, block_ones, scale, queries, q_at, keys, values, at):
    parts = [project(w, layer, block, wide, block_ones, keys, at) for block in (2, 3)]
    parts += [project(w, layer, block, narrow, block_ones, queries, q_at, scale) for block in (0, 1)]
    return parts + [project(w, layer, block, wide, block_ones, values, at, plain=True) for block in (4, 5)]


def query_lanes(table):
    r = lax.axis_index("rad")
    lane = lax.broadcasted_iota(jnp.int32, (1, 128), 1)
    ends = ((lane == 48) & (r == 0)) | ((lane == 49) & (r == lax.axis_size("rad") - 1))
    return table + jnp.where(ends, 1.0, 0.0).astype(jnp.bfloat16)


def attend(queries, query_aug, keys, key_aug, values, att):
    n = query_aug.shape[0]
    lane = lax.broadcasted_iota(jnp.int32, (1, 128), 1)
    low = jnp.where(lane < 64, 1.0, 0.0).astype(jnp.bfloat16)
    high = jnp.where(lane < 64, 0.0, 1.0).astype(jnp.bfloat16)
    half = lax.broadcasted_iota(jnp.int32, (n, 128), 1) < 64
    one = jnp.ones((key_aug.shape[0], 128), jnp.bfloat16)

    def pair_of_heads(pair):
        lanes = slice(pair * 128, pair * 128 + 128)

        def rows(parts):
            return jnp.concatenate([ref[at : at + count, lanes] for ref, at, count in parts], axis=0)

        q = rows(queries)
        q = jnp.concatenate(
            [jnp.concatenate([q * low, query_aug], axis=1), jnp.concatenate([q * high, query_aug], axis=1)], axis=0
        )
        k = jnp.concatenate([rows(keys), key_aug], axis=1)
        score = lax.dot_general(q, k, (((1,), (1,)), ((), ())), preferred_element_type=jnp.float32)
        yield
        got = dot(jnp.exp2(score).astype(jnp.bfloat16), jnp.concatenate([rows(values), one], axis=1))
        yield
        top = jnp.where(half, got[:n, :128], got[n:, :128])
        total = jnp.where(half, got[:n, 128:], got[n:, 128:])
        att[0:n, lanes] = (top / total).astype(jnp.bfloat16)

    return [pair_of_heads(pair) for pair in range(HEADS // 2)]


def columns(x, at, count, width):
    return x[at : at + count, :width].reshape(count * width, WIDTH)


def inner_kernel(
    first, second, scale, gains, w_qkv, w_out, block_ones, q_aug, k_aug,
    queries, keys, values, stream, queries_1, keys_1, values_1, att,
):
    x = jnp.concatenate([first[...], second[...]], axis=0).astype(jnp.float32)
    normed = norm_rows(x.reshape(512, WIDTH), gains[0:1, :])
    narrow = columns(normed.reshape(16, 32, WIDTH), 0, 16, 24).astype(jnp.bfloat16)
    wide = normed.astype(jnp.bfloat16)
    interleave(project_all(w_qkv, 0, wide, narrow, block_ones, scale, queries, 0, keys, values, 0), 2)
    pairs = attend(
        [(queries, 96, 192)], query_lanes(q_aug[192:384]), [(keys, 0, 512)], k_aug[256:768], [(values, 0, 512)], att
    )
    interleave(pairs, 2)
    x = rounded(columns(x, 4, 8, 24) + dot(att[...], w_out[0]))
    stream[...] = x.astype(jnp.bfloat16)
    normed = norm_rows(x, gains[1:2, :])
    narrow = columns(normed.reshape(8, 24, WIDTH), 0, 8, 16).astype(jnp.bfloat16)
    wide = normed.astype(jnp.bfloat16)
    interleave(project_all(w_qkv, 1, wide, narrow, block_ones, scale, queries_1, 0, keys_1, values_1, 0), 2)


def inner(*arrays):
    outs = [(384, WIDTH), (512, WIDTH), (512, WIDTH), (192, WIDTH), (128, WIDTH), (192, WIDTH), (192, WIDTH)]
    scratch = [pltpu.VMEM((192, WIDTH), jnp.bfloat16)]
    return call(inner_kernel, "inner", outs, [VMEM] * 9, scratch=scratch, mib=14)(*arrays)


def outer_kernel(
    low, high, first, second, scale, gains, w_qkv, w_out, last_gain, block_ones, q_aug, k_aug, q_aug_1, k_aug_1,
    q_mid, k_mid, v_mid, stream_mid, q1_mid, k1_mid, v1_mid,
    out, q_end, k_end, v_end, q1_end, k1_end, v1_end, att_0, att_1,
):
    att = (att_0, att_1)
    x = jnp.concatenate([low[...], high[...]], axis=0).astype(jnp.float32)
    normed = norm_rows(x.reshape(512, WIDTH), gains[0:1, :])
    narrow = columns(normed.reshape(16, 32, WIDTH), 4, 8, 24).astype(jnp.bfloat16)
    wide = normed.astype(jnp.bfloat16)
    interleave(project_all(w_qkv, 0, wide, narrow, block_ones, scale, q_end, 0, k_end, v_end, 0), 2)
    pairs = []
    for part in range(2):
        if part == 0:
            q = [(q_end, 0, 96), (q_mid, 0, 96)]
            k, v = [[(end, 0, 256), (mid, 0, 256)] for end, mid in ((k_end, k_mid), (v_end, v_mid))]
        else:
            q = [(q_mid, 288, 96), (q_end, 96, 96)]
            k, v = [[(mid, 256, 256), (end, 256, 256)] for end, mid in ((k_end, k_mid), (v_end, v_mid))]
        q_lanes = query_lanes(q_aug[384 * part : 384 * part + 192])
        pairs.append(attend(q, q_lanes, k, k_aug[512 * part : 512 * part + 512], v, att[part]))
    kept = [None, None]

    def finish(part):
        at = 4 * (1 - part)
        ours = first if part == 0 else second
        before = [columns(x, 4 + 4 * part, 4, 24), columns(ours[...].astype(jnp.float32), 4 * part, 4, 24)]
        y = dot(att[part][...], w_out[0])
        yield
        y = rounded(jnp.concatenate(before if part == 0 else before[::-1], axis=0) + y)
        normed = norm_rows(y, gains[1:2, :])
        narrow = columns(normed.reshape(8, 24, WIDTH), at, 4, 16).astype(jnp.bfloat16)
        kept[part] = columns(y.reshape(8, 24, WIDTH), at, 4, 16)
        yield
        wide = normed.astype(jnp.bfloat16)
        yield from one_by_one(
            *project_all(
                w_qkv, 1, wide, narrow, block_ones, scale, q1_end, 64 * part, k1_end, v1_end, 192 * part
            )
        )

    interleave(pairs[0], 2)
    interleave([one_by_one(*pairs[1]), finish(0)], 2)
    middle = stream_mid[...].astype(jnp.float32).reshape(8, 24, WIDTH)
    pairs = []
    for part in range(2):
        if part == 0:
            q = [(q1_end, 0, 64), (q1_mid, 0, 64)]
            k, v = [[(end, 0, 192), (mid, 0, 192)] for end, mid in ((k1_end, k1_mid), (v1_end, v1_mid))]
        else:
            q = [(q1_mid, 64, 64), (q1_end, 64, 64)]
            k, v = [[(mid, 0, 192), (end, 192, 192)] for end, mid in ((k1_end, k1_mid), (v1_end, v1_mid))]
        q_lanes = query_lanes(q_aug_1[128 * part : 128 * part + 128])
        pairs.append(attend(q, q_lanes, k, k_aug_1[192 * part : 192 * part + 384], v, att[part]))

    def end(part):
        before = [columns(middle, 4 * part, 4, 16), kept[part]]
        y = dot(att[part][0:128], w_out[1])
        yield
        y = rounded(jnp.concatenate(before if part else before[::-1], axis=0) + y)
        latent = norm_rows(y, last_gain[...])
        out[8 * part : 8 * part + 8] = latent.reshape(8, 16, WIDTH).astype(jnp.bfloat16)

    interleave([finish(1), one_by_one(*pairs[0])], 2)
    interleave([one_by_one(*pairs[1]), end(0)], 2)
    interleave([end(1)], 1)


def outer(*arrays):
    scratch = [192, 512, 512, 128, 384, 384, 192, 192]
    return call(
        outer_kernel,
        "outer",
        [(16, 16, WIDTH)],
        [VMEM] * 21,
        scratch=[pltpu.VMEM((rows, WIDTH), jnp.bfloat16) for rows in scratch],
        mib=14,
    )(*arrays)[0]


def swap(x, shift):
    count = lax.axis_size("rad")
    pairs = [(i, ((i + shift) ^ 1) - shift) for i in range(count)]
    return lax.ppermute(x, "rad", [(i, j) for i, j in pairs if 0 <= j < count])


def pass_on(x, step):
    count = lax.axis_size("az")
    return lax.ppermute(x, "az", [(i, (i + step) % count) for i in range(count)])


def per_device(
    hidden_site_vector,
    mesh_portion_descriptors,
    mesh_entry_site,
    mesh_portion_tally,
    incline_grid_position,
    incline_vector_lookup,
    mesh_mapping_matrix,
    prefocus_rescale_factor,
    probe_lock_payload_matrix,
    sharpness_scale,
    final_mapping_matrix,
    terminal_rescale_factor,
):
    packed, token = pack(
        mesh_portion_descriptors.reshape(128, 16, 128), mesh_entry_site.reshape(16, 128), mesh_portion_tally
    )
    arrived = lax.all_to_all(packed, ("az", "rad"), split_axis=0, concat_axis=0, tiled=True)

    hidden = hidden_site_vector[0]
    block_ones = jnp.asarray(np.kron(np.eye(4), np.ones((64, 64))), jnp.bfloat16)
    pitch, scale, to_a, to_b = stage(
        token, incline_grid_position, sharpness_scale, incline_vector_lookup, hidden
    )
    hid_a, hid_b = swap(to_a, 0), swap(to_b, 1)

    feat, to_a, to_b = cell_sums(arrived)
    feat_a, feat_b = swap(to_a, 0), swap(to_b, 1)
    first, second = band(feat, feat_a, feat_b, hidden, hid_a, hid_b, pitch, mesh_mapping_matrix)
    low, high = pass_on(second, 1), pass_on(first, -1)
    q_aug, k_aug, q_aug_1, k_aug_1 = window_tables()
    weights = (scale, prefocus_rescale_factor, probe_lock_payload_matrix, final_mapping_matrix)
    middle = inner(first, second, *weights, block_ones, q_aug, k_aug)
    out = outer(
        low, high, first, second, *weights, terminal_rescale_factor[None, :],
        block_ones, q_aug, k_aug, q_aug_1, k_aug_1, *middle,
    )
    return out[None]


def solution(mesh):
    rows = P(("az", "rad"), None)
    in_specs = (P(None, "az", "rad", None), rows, P(("az", "rad")), rows) + (P(),) * 8
    return jax.shard_map(
        per_device,
        mesh=mesh,
        in_specs=in_specs,
        out_specs=P(None, "az", "rad", None),
        check_vma=False,
    )
```

```python
import jax
import jax.numpy as jnp
import numpy as np
from jax import lax
from jax.experimental import pallas as pl
from jax.experimental.pallas import tpu as pltpu
from jax.sharding import PartitionSpec as P

HALO = 4
HEADS = 8
WIDTH = 512
EDGE = 2 * HALO
DEAD = 256
NEG = -1024.0
LOG2E = 1.4426950408889634
COLUMN_J = np.array(
    list(range(8, 24)) + list(range(24, 28)) + list(range(4, 8)) + list(range(0, 4)) + list(range(28, 32))
)
SMEM = pl.BlockSpec(memory_space=pltpu.SMEM)
VMEM = pl.BlockSpec(memory_space=pltpu.VMEM)
HBM = pl.BlockSpec(memory_space=pltpu.HBM)


def window_tables():
    i = np.arange(32)
    key = np.zeros((32, 32, 128), np.float32)
    query = np.zeros((24, 24, 128), np.float32)
    for d in range(24):
        key[:, :, d] = np.where(np.abs(COLUMN_J - COLUMN_J[d]) > HALO, NEG, 0.0)[None, :]
        key[:, :, 24 + d] = np.where(np.abs(i - (d + HALO)) > HALO, NEG, 0.0)[:, None]
        query[:, d, d] = 1.0
        query[d, :, 24 + d] = 1.0
    key[:, :, 48] = np.where(COLUMN_J < 8, NEG, 0.0)[None, :]
    key[:, :, 49] = np.where(COLUMN_J >= 24, NEG, 0.0)[None, :]
    tables = (
        query.reshape(576, 128),
        key.reshape(1024, 128),
        query[4:20, :16].reshape(256, 128),
        key[4:28, :24].reshape(576, 128),
    )
    return [jnp.asarray(t, jnp.bfloat16) for t in tables]


def dot(a, b):
    return jnp.dot(a, b, preferred_element_type=jnp.float32)


def rounded(x):
    return x.astype(jnp.bfloat16).astype(jnp.float32)


def norm_rows(x, gain):
    return x * lax.rsqrt(jnp.mean(x * x, -1, keepdims=True) + 1e-05) * gain


def shape_of(x):
    return x if isinstance(x, jax.ShapeDtypeStruct) else jax.ShapeDtypeStruct(x, jnp.bfloat16)


COST = {"pack": 1.5, "stage": 1, "cell_sums": 2, "band": 1.5, "inner": 4, "outer": 8}


def call(kernel, name, outs, in_specs, out_specs=None, scratch=(), mib=8):
    return pl.pallas_call(
        kernel,
        out_shape=[shape_of(x) for x in outs],
        in_specs=in_specs,
        out_specs=out_specs or [VMEM] * len(outs),
        scratch_shapes=scratch,
        compiler_params=pltpu.CompilerParams(vmem_limit_bytes=mib << 20),
        name=name,
        cost_estimate=pl.CostEstimate(
            flops=int(COST[name] * 1e9), bytes_accessed=int(COST[name] * 3e6), transcendentals=0
        ),
    )


def interleave(tasks, depth):
    waiting = list(tasks)
    active = []
    while waiting or active:
        if waiting and len(active) < depth:
            active.append(waiting.pop(0))
        for task in list(active):
            if next(task, True):
                active.remove(task)


def one_by_one(*tasks):
    for task in tasks:
        yield from task


def pack_kernel(rows, cells, tally, packed, token, block, cells_here, tally_here, sems, out_sem):
    ids_load = pltpu.make_async_copy(cells, cells_here, sems.at[8])
    tally_load = pltpu.make_async_copy(tally, tally_here, sems.at[9])
    ids_load.start()
    tally_load.start()
    loads = [
        pltpu.make_async_copy(rows.at[:, k], block.at[:, :, pl.ds(128 * k, 128)], sems.at[k]) for k in range(8)
    ]
    for load in loads:
        load.start()
    t = lax.broadcasted_iota(jnp.int32, (128, 128), 0)
    lane = lax.broadcasted_iota(jnp.int32, (128, 128), 1)
    mine = t % 8 == lane // 16
    slot = lane % 16
    pick = jnp.where(mine, 1.0, 0.0).astype(jnp.bfloat16)
    r = lax.axis_index("rad")
    order = (lane // 16 == t % 16 // 2) & (lane % 16 == 2 * r + t % 2)
    order = jnp.where(order, 1.0, 0.0).astype(jnp.bfloat16)
    ids_load.wait()
    tally_load.wait()
    here = lax.broadcasted_iota(jnp.int32, (16, 128), 1) // 8 == lax.broadcasted_iota(jnp.int32, (16, 128), 0)
    spread = jnp.where(here, tally_here[...].astype(jnp.float32), 0.0).astype(jnp.bfloat16)
    live = slot[:16].astype(jnp.float32) < dot(spread, pick)
    ids = jnp.where(live, cells_here[...].astype(jnp.float32), float(DEAD))
    ids = jnp.broadcast_to(ids[:, None, :], (16, 8, 128)).reshape(128, 128)
    ids = dot(jnp.where(mine, ids, 0.0).astype(jnp.bfloat16), order)
    for at in range(128):
        block[at, :, 1024:1152] = jnp.broadcast_to(ids[at : at + 1], (2, 128)).astype(jnp.bfloat16)
    for load in loads:
        load.wait()
    store = pltpu.make_async_copy(block, packed, out_sem)
    store.start()
    token[...] = jnp.zeros((8, 128), jnp.float32)
    store.wait()


def pack(rows, cells, tally):
    return call(
        pack_kernel,
        "pack",
        [(128, 2, 1152), jax.ShapeDtypeStruct((8, 128), jnp.float32)],
        [HBM] * 3,
        [HBM, VMEM],
        [
            pltpu.VMEM((128, 2, 1152), jnp.bfloat16),
            pltpu.VMEM((16, 128), jnp.int32),
            pltpu.VMEM((1, 128), jnp.int32),
            pltpu.SemaphoreType.DMA((10,)),
            pltpu.SemaphoreType.DMA,
        ],
        mib=60,
    )(rows, cells, tally)


def stage_kernel(token, pitch_at, sharp, lookup, hidden, pitch, scale, send_a, send_b):
    rows = lax.broadcasted_iota(jnp.int32, (64, 1), 0)
    pitch[...] = jnp.sum(
        jnp.where(rows == pitch_at[0], lookup[...].astype(jnp.float32), 0.0), axis=0, keepdims=True
    )
    head = lax.broadcasted_iota(jnp.int32, (1, WIDTH), 1) // 64
    for layer in range(2):
        line = token[0:1, 0:1] * jnp.ones((1, WIDTH), jnp.float32)
        for h in range(HEADS):
            line = jnp.where(head == h, sharp[layer, h] * LOG2E, line)
        scale[layer : layer + 1] = line
    even = lax.rem(lax.axis_index("rad"), 2) == 0
    low = hidden[:, :EDGE].astype(jnp.float32)
    high = hidden[:, EDGE:].astype(jnp.float32)
    send_a[...] = jnp.where(even, high, low).astype(jnp.bfloat16)
    send_b[...] = jnp.where(even, low, high).astype(jnp.bfloat16)


def stage(*arrays):
    edge = (16, EDGE, WIDTH)
    row = jax.ShapeDtypeStruct((1, WIDTH), jnp.float32)
    two = jax.ShapeDtypeStruct((2, WIDTH), jnp.float32)
    return call(stage_kernel, "stage", [row, two, edge, edge], [VMEM, SMEM, SMEM, VMEM, VMEM])(*arrays)


def cell_sum_kernel(block, feat, send_a, send_b):
    cell = lax.broadcasted_iota(jnp.int32, (256, 128), 0).astype(jnp.float32)
    total = jnp.zeros((256, 128), jnp.float32)
    ids = jnp.sum(block[:, :, 1024:1152].astype(jnp.float32).reshape(16, 8, 2, 128), axis=1)
    for step in range(4):
        picks = []
        rows = []
        for part in range(4 * step, 4 * step + 4):
            wide = jnp.broadcast_to(ids[part, 0:1], (256, 128))
            picks.append(jnp.where(wide == cell, 1.0, 0.0).astype(jnp.bfloat16))
            rows += [block[8 * part : 8 * part + 8, :, 128 * k : 128 * k + 128].reshape(16, 128) for k in range(8)]
        total = total + dot(jnp.concatenate(picks, axis=1), jnp.concatenate(rows, axis=0))
    total = rounded(total).reshape(16, 16, 128)
    feat[...] = total.astype(jnp.bfloat16)
    even = lax.rem(lax.axis_index("rad"), 2) == 0
    low = total[:, :EDGE]
    high = total[:, EDGE:]
    send_a[...] = jnp.where(even, high, low).astype(jnp.bfloat16)
    send_b[...] = jnp.where(even, low, high).astype(jnp.bfloat16)


def cell_sums(arrived):
    return call(
        cell_sum_kernel,
        "cell_sums",
        [(16, 16, 128), (16, EDGE, 128), (16, EDGE, 128)],
        [VMEM],
    )(arrived)


def band_kernel(feat, feat_a, feat_b, hid, hid_a, hid_b, pitch, w_map, first, second):
    even = lax.rem(lax.axis_index("rad"), 2) == 0

    def wide(own, got_a, got_b, at):
        here = slice(at, at + 8)
        a = got_a[here].astype(jnp.float32)
        b = got_b[here].astype(jnp.float32)
        from_a = (lax.broadcasted_iota(jnp.int32, a.shape, 1) < HALO) == even
        parts = [own[here].astype(jnp.float32), jnp.where(from_a, a, b), jnp.where(from_a, b, a)]
        return jnp.concatenate(parts, axis=1).reshape(256, a.shape[-1])

    for at, out in ((0, first), (8, second)):
        x = dot(wide(feat, feat_a, feat_b, at).astype(jnp.bfloat16), w_map[...])
        x = wide(hid, hid_a, hid_b, at) + x + pitch[...]
        out[...] = x.reshape(8, 32, WIDTH).astype(jnp.bfloat16)


def band(*arrays):
    return call(band_kernel, "band", [(EDGE, 32, WIDTH)] * 2, [VMEM] * 8)(*arrays)


def project(w, layer, block, rows, block_ones, target, at, scale=None, plain=False):
    x = dot(rows, w[layer, :, block * 256 : block * 256 + 256])
    lanes = slice(block % 2 * 256, block % 2 * 256 + 256)
    yield
    if not plain:
        x = rounded(x)
        squares = dot((x * x).astype(jnp.bfloat16), block_ones[...])
        yield
        x = x * lax.rsqrt(squares + 1e-06)
    if scale is not None:
        x = x * scale[layer : layer + 1, lanes]
    target[at : at + x.shape[0], lanes] = x.astype(jnp.bfloat16)


def project_all(w, layer, wide, narrow, block_ones, scale, queries, q_at, keys, values, at):
    parts = [project(w, layer, block, wide, block_ones, keys, at) for block in (2, 3)]
    parts += [project(w, layer, block, narrow, block_ones, queries, q_at, scale) for block in (0, 1)]
    return parts + [project(w, layer, block, wide, block_ones, values, at, plain=True) for block in (4, 5)]


def query_lanes(table):
    r = lax.axis_index("rad")
    lane = lax.broadcasted_iota(jnp.int32, (1, 128), 1)
    ends = ((lane == 48) & (r == 0)) | ((lane == 49) & (r == lax.axis_size("rad") - 1))
    return table + jnp.where(ends, 1.0, 0.0).astype(jnp.bfloat16)


def attend(queries, query_aug, keys, key_aug, values, att):
    n = query_aug.shape[0]
    lane = lax.broadcasted_iota(jnp.int32, (1, 128), 1)
    low = jnp.where(lane < 64, 1.0, 0.0).astype(jnp.bfloat16)
    high = jnp.where(lane < 64, 0.0, 1.0).astype(jnp.bfloat16)
    half = lax.broadcasted_iota(jnp.int32, (n, 128), 1) < 64
    one = jnp.ones((key_aug.shape[0], 128), jnp.bfloat16)

    def pair_of_heads(pair):
        lanes = slice(pair * 128, pair * 128 + 128)

        def rows(parts):
            return jnp.concatenate([ref[at : at + count, lanes] for ref, at, count in parts], axis=0)

        q = rows(queries)
        q = jnp.concatenate(
            [jnp.concatenate([q * low, query_aug], axis=1), jnp.concatenate([q * high, query_aug], axis=1)], axis=0
        )
        k = jnp.concatenate([rows(keys), key_aug], axis=1)
        score = lax.dot_general(q, k, (((1,), (1,)), ((), ())), preferred_element_type=jnp.float32)
        yield
        got = dot(jnp.exp2(score).astype(jnp.bfloat16), jnp.concatenate([rows(values), one], axis=1))
        yield
        top = jnp.where(half, got[:n, :128], got[n:, :128])
        total = jnp.where(half, got[:n, 128:], got[n:, 128:])
        att[0:n, lanes] = (top / total).astype(jnp.bfloat16)

    return [pair_of_heads(pair) for pair in range(HEADS // 2)]


def columns(x, at, count, width):
    return x[at : at + count, :width].reshape(count * width, WIDTH)


def inner_kernel(
    first, second, scale, gains, w_qkv, w_out, block_ones, q_aug, k_aug,
    queries, keys, values, stream, queries_1, keys_1, values_1, att,
):
    x = jnp.concatenate([first[...], second[...]], axis=0).astype(jnp.float32)
    normed = norm_rows(x.reshape(512, WIDTH), gains[0:1, :])
    narrow = columns(normed.reshape(16, 32, WIDTH), 0, 16, 24).astype(jnp.bfloat16)
    wide = normed.astype(jnp.bfloat16)
    interleave(project_all(w_qkv, 0, wide, narrow, block_ones, scale, queries, 0, keys, values, 0), 2)
    pairs = attend(
        [(queries, 96, 192)], query_lanes(q_aug[192:384]), [(keys, 0, 512)], k_aug[256:768], [(values, 0, 512)], att
    )
    interleave(pairs, 2)
    x = rounded(columns(x, 4, 8, 24) + dot(att[...], w_out[0]))
    stream[...] = x.astype(jnp.bfloat16)
    normed = norm_rows(x, gains[1:2, :])
    narrow = columns(normed.reshape(8, 24, WIDTH), 0, 8, 16).astype(jnp.bfloat16)
    wide = normed.astype(jnp.bfloat16)
    interleave(project_all(w_qkv, 1, wide, narrow, block_ones, scale, queries_1, 0, keys_1, values_1, 0), 2)


def inner(*arrays):
    outs = [(384, WIDTH), (512, WIDTH), (512, WIDTH), (192, WIDTH), (128, WIDTH), (192, WIDTH), (192, WIDTH)]
    scratch = [pltpu.VMEM((192, WIDTH), jnp.bfloat16)]
    return call(inner_kernel, "inner", outs, [VMEM] * 9, scratch=scratch, mib=14)(*arrays)


def outer_kernel(
    low, high, first, second, scale, gains, w_qkv, w_out, last_gain, block_ones, q_aug, k_aug, q_aug_1, k_aug_1,
    q_mid, k_mid, v_mid, stream_mid, q1_mid, k1_mid, v1_mid,
    out, q_end, k_end, v_end, q1_end, k1_end, v1_end, att_0, att_1,
):
    att = (att_0, att_1)
    x = jnp.concatenate([low[...], high[...]], axis=0).astype(jnp.float32)
    normed = norm_rows(x.reshape(512, WIDTH), gains[0:1, :])
    narrow = columns(normed.reshape(16, 32, WIDTH), 4, 8, 24).astype(jnp.bfloat16)
    wide = normed.astype(jnp.bfloat16)
    interleave(project_all(w_qkv, 0, wide, narrow, block_ones, scale, q_end, 0, k_end, v_end, 0), 2)
    pairs = []
    for part in range(2):
        if part == 0:
            q = [(q_end, 0, 96), (q_mid, 0, 96)]
            k, v = [[(end, 0, 256), (mid, 0, 256)] for end, mid in ((k_end, k_mid), (v_end, v_mid))]
        else:
            q = [(q_mid, 288, 96), (q_end, 96, 96)]
            k, v = [[(mid, 256, 256), (end, 256, 256)] for end, mid in ((k_end, k_mid), (v_end, v_mid))]
        q_lanes = query_lanes(q_aug[384 * part : 384 * part + 192])
        pairs.append(attend(q, q_lanes, k, k_aug[512 * part : 512 * part + 512], v, att[part]))
    kept = [None, None]

    def finish(part):
        at = 4 * (1 - part)
        ours = first if part == 0 else second
        before = [columns(x, 4 + 4 * part, 4, 24), columns(ours[...].astype(jnp.float32), 4 * part, 4, 24)]
        y = dot(att[part][...], w_out[0])
        yield
        y = rounded(jnp.concatenate(before if part == 0 else before[::-1], axis=0) + y)
        normed = norm_rows(y, gains[1:2, :])
        narrow = columns(normed.reshape(8, 24, WIDTH), at, 4, 16).astype(jnp.bfloat16)
        kept[part] = columns(y.reshape(8, 24, WIDTH), at, 4, 16)
        yield
        wide = normed.astype(jnp.bfloat16)
        yield from one_by_one(
            *project_all(
                w_qkv, 1, wide, narrow, block_ones, scale, q1_end, 64 * part, k1_end, v1_end, 192 * part
            )
        )

    interleave(pairs[0], 2)
    interleave([one_by_one(*pairs[1]), finish(0)], 2)
    middle = stream_mid[...].astype(jnp.float32).reshape(8, 24, WIDTH)
    pairs = []
    for part in range(2):
        if part == 0:
            q = [(q1_end, 0, 64), (q1_mid, 0, 64)]
            k, v = [[(end, 0, 192), (mid, 0, 192)] for end, mid in ((k1_end, k1_mid), (v1_end, v1_mid))]
        else:
            q = [(q1_mid, 64, 64), (q1_end, 64, 64)]
            k, v = [[(mid, 0, 192), (end, 192, 192)] for end, mid in ((k1_end, k1_mid), (v1_end, v1_mid))]
        q_lanes = query_lanes(q_aug_1[128 * part : 128 * part + 128])
        pairs.append(attend(q, q_lanes, k, k_aug_1[192 * part : 192 * part + 384], v, att[part]))

    def end(part):
        before = [columns(middle, 4 * part, 4, 16), kept[part]]
        y = dot(att[part][0:128], w_out[1])
        yield
        y = rounded(jnp.concatenate(before if part else before[::-1], axis=0) + y)
        latent = norm_rows(y, last_gain[...])
        out[8 * part : 8 * part + 8] = latent.reshape(8, 16, WIDTH).astype(jnp.bfloat16)

    interleave([finish(1), one_by_one(*pairs[0])], 2)
    interleave([one_by_one(*pairs[1]), end(0)], 2)
    interleave([end(1)], 1)


def outer(*arrays):
    scratch = [192, 512, 512, 128, 384, 384, 192, 192]
    return call(
        outer_kernel,
        "outer",
        [(16, 16, WIDTH)],
        [VMEM] * 21,
        scratch=[pltpu.VMEM((rows, WIDTH), jnp.bfloat16) for rows in scratch],
        mib=14,
    )(*arrays)[0]


def swap(x, shift):
    count = lax.axis_size("rad")
    pairs = [(i, ((i + shift) ^ 1) - shift) for i in range(count)]
    return lax.ppermute(x, "rad", [(i, j) for i, j in pairs if 0 <= j < count])


def pass_on(x, step):
    count = lax.axis_size("az")
    return lax.ppermute(x, "az", [(i, (i + step) % count) for i in range(count)])


def per_device(
    hidden_site_vector,
    mesh_portion_descriptors,
    mesh_entry_site,
    mesh_portion_tally,
    incline_grid_position,
    incline_vector_lookup,
    mesh_mapping_matrix,
    prefocus_rescale_factor,
    probe_lock_payload_matrix,
    sharpness_scale,
    final_mapping_matrix,
    terminal_rescale_factor,
):
    packed, token = pack(
        mesh_portion_descriptors.reshape(128, 8, 2, 128), mesh_entry_site.reshape(16, 128), mesh_portion_tally
    )
    arrived = lax.all_to_all(packed, ("az", "rad"), split_axis=0, concat_axis=0, tiled=True)

    hidden = hidden_site_vector[0]
    block_ones = jnp.asarray(np.kron(np.eye(4), np.ones((64, 64))), jnp.bfloat16)
    pitch, scale, to_a, to_b = stage(
        token, incline_grid_position, sharpness_scale, incline_vector_lookup, hidden
    )
    hid_a, hid_b = swap(to_a, 0), swap(to_b, 1)

    feat, to_a, to_b = cell_sums(arrived)
    feat_a, feat_b = swap(to_a, 0), swap(to_b, 1)
    first, second = band(feat, feat_a, feat_b, hidden, hid_a, hid_b, pitch, mesh_mapping_matrix)
    low, high = pass_on(second, 1), pass_on(first, -1)
    q_aug, k_aug, q_aug_1, k_aug_1 = window_tables()
    weights = (scale, prefocus_rescale_factor, probe_lock_payload_matrix, final_mapping_matrix)
    middle = inner(first, second, *weights, block_ones, q_aug, k_aug)
    out = outer(
        low, high, first, second, *weights, terminal_rescale_factor[None, :],
        block_ones, q_aug, k_aug, q_aug_1, k_aug_1, *middle,
    )
    return out[None]


def solution(mesh):
    rows = P(("az", "rad"), None)
    in_specs = (P(None, "az", "rad", None), rows, P(("az", "rad")), rows) + (P(),) * 8
    return jax.shard_map(
        per_device,
        mesh=mesh,
        in_specs=in_specs,
        out_specs=P(None, "az", "rad", None),
        check_vma=False,
    )
```

```python
import jax
import jax.numpy as jnp
import numpy as np
from jax import lax
from jax.experimental import pallas as pl
from jax.experimental.pallas import tpu as pltpu
from jax.sharding import PartitionSpec as P

HALO = 4
HEADS = 8
WIDTH = 512
EDGE = 2 * HALO
DEAD = 256
NEG = -1024.0
LOG2E = 1.4426950408889634
COLUMN_J = np.array(
    list(range(8, 24)) + list(range(24, 28)) + list(range(4, 8)) + list(range(0, 4)) + list(range(28, 32))
)
SMEM = pl.BlockSpec(memory_space=pltpu.SMEM)
VMEM = pl.BlockSpec(memory_space=pltpu.VMEM)
HBM = pl.BlockSpec(memory_space=pltpu.HBM)


def window_tables():
    i = np.arange(32)
    key = np.zeros((32, 32, 128), np.float32)
    query = np.zeros((24, 24, 128), np.float32)
    for d in range(24):
        key[:, :, d] = np.where(np.abs(COLUMN_J - COLUMN_J[d]) > HALO, NEG, 0.0)[None, :]
        key[:, :, 24 + d] = np.where(np.abs(i - (d + HALO)) > HALO, NEG, 0.0)[:, None]
        query[:, d, d] = 1.0
        query[d, :, 24 + d] = 1.0
    key[:, :, 48] = np.where(COLUMN_J < 8, NEG, 0.0)[None, :]
    key[:, :, 49] = np.where(COLUMN_J >= 24, NEG, 0.0)[None, :]
    tables = (
        query.reshape(576, 128),
        key.reshape(1024, 128),
        query[4:20, :16].reshape(256, 128),
        key[4:28, :24].reshape(576, 128),
    )
    return [jnp.asarray(t, jnp.bfloat16) for t in tables]


def dot(a, b):
    return jnp.dot(a, b, preferred_element_type=jnp.float32)


def rounded(x):
    return x.astype(jnp.bfloat16).astype(jnp.float32)


def norm_rows(x, gain):
    return x * lax.rsqrt(jnp.mean(x * x, -1, keepdims=True) + 1e-05) * gain


def shape_of(x):
    return x if isinstance(x, jax.ShapeDtypeStruct) else jax.ShapeDtypeStruct(x, jnp.bfloat16)


COST = {"pack": 1.5, "stage": 1, "cell_sums": 2, "band": 1, "widen": 1, "inner": 4, "outer": 8}


def call(kernel, name, outs, in_specs, out_specs=None, scratch=(), mib=8):
    return pl.pallas_call(
        kernel,
        out_shape=[shape_of(x) for x in outs],
        in_specs=in_specs,
        out_specs=out_specs or [VMEM] * len(outs),
        scratch_shapes=scratch,
        compiler_params=pltpu.CompilerParams(vmem_limit_bytes=mib << 20),
        name=name,
        cost_estimate=pl.CostEstimate(
            flops=int(COST[name] * 1e9), bytes_accessed=int(COST[name] * 3e6), transcendentals=0
        ),
    )


def interleave(tasks, depth):
    waiting = list(tasks)
    active = []
    while waiting or active:
        if waiting and len(active) < depth:
            active.append(waiting.pop(0))
        for task in list(active):
            if next(task, True):
                active.remove(task)


def one_by_one(*tasks):
    for task in tasks:
        yield from task


def pack_kernel(rows, cells, tally, packed, token, block, cells_here, tally_here, sems, out_sem):
    ids_load = pltpu.make_async_copy(cells, cells_here, sems.at[8])
    tally_load = pltpu.make_async_copy(tally, tally_here, sems.at[9])
    ids_load.start()
    tally_load.start()
    loads = [
        pltpu.make_async_copy(rows.at[:, k], block.at[:, :, pl.ds(128 * k, 128)], sems.at[k]) for k in range(8)
    ]
    for load in loads:
        load.start()
    t = lax.broadcasted_iota(jnp.int32, (128, 128), 0)
    lane = lax.broadcasted_iota(jnp.int32, (128, 128), 1)
    mine = t % 8 == lane // 16
    slot = lane % 16
    pick = jnp.where(mine, 1.0, 0.0).astype(jnp.bfloat16)
    r = lax.axis_index("rad")
    order = (lane // 16 == t % 16 // 2) & (lane % 16 == 2 * r + t % 2)
    order = jnp.where(order, 1.0, 0.0).astype(jnp.bfloat16)
    ids_load.wait()
    tally_load.wait()
    here = lax.broadcasted_iota(jnp.int32, (16, 128), 1) // 8 == lax.broadcasted_iota(jnp.int32, (16, 128), 0)
    spread = jnp.where(here, tally_here[...].astype(jnp.float32), 0.0).astype(jnp.bfloat16)
    live = slot[:16].astype(jnp.float32) < dot(spread, pick)
    ids = jnp.where(live, cells_here[...].astype(jnp.float32), float(DEAD))
    ids = jnp.broadcast_to(ids[:, None, :], (16, 8, 128)).reshape(128, 128)
    ids = dot(jnp.where(mine, ids, 0.0).astype(jnp.bfloat16), order)
    for at in range(128):
        block[at, :, 1024:1152] = jnp.broadcast_to(ids[at : at + 1], (2, 128)).astype(jnp.bfloat16)
    for load in loads:
        load.wait()
    store = pltpu.make_async_copy(block, packed, out_sem)
    store.start()
    token[...] = jnp.zeros((8, 128), jnp.float32)
    store.wait()


def pack(rows, cells, tally):
    return call(
        pack_kernel,
        "pack",
        [(128, 2, 1152), jax.ShapeDtypeStruct((8, 128), jnp.float32)],
        [HBM] * 3,
        [HBM, VMEM],
        [
            pltpu.VMEM((128, 2, 1152), jnp.bfloat16),
            pltpu.VMEM((16, 128), jnp.int32),
            pltpu.VMEM((1, 128), jnp.int32),
            pltpu.SemaphoreType.DMA((10,)),
            pltpu.SemaphoreType.DMA,
        ],
        mib=60,
    )(rows, cells, tally)


def stage_kernel(token, pitch_at, sharp, lookup, hidden, pitch, scale, send_a, send_b):
    rows = lax.broadcasted_iota(jnp.int32, (64, 1), 0)
    pitch[...] = jnp.sum(
        jnp.where(rows == pitch_at[0], lookup[...].astype(jnp.float32), 0.0), axis=0, keepdims=True
    )
    head = lax.broadcasted_iota(jnp.int32, (1, WIDTH), 1) // 64
    for layer in range(2):
        line = token[0:1, 0:1] * jnp.ones((1, WIDTH), jnp.float32)
        for h in range(HEADS):
            line = jnp.where(head == h, sharp[layer, h] * LOG2E, line)
        scale[layer : layer + 1] = line
    even = lax.rem(lax.axis_index("rad"), 2) == 0
    low = hidden[:, :EDGE].astype(jnp.float32)
    high = hidden[:, EDGE:].astype(jnp.float32)
    send_a[...] = jnp.where(even, high, low).astype(jnp.bfloat16)
    send_b[...] = jnp.where(even, low, high).astype(jnp.bfloat16)


def stage(*arrays):
    edge = (16, EDGE, WIDTH)
    row = jax.ShapeDtypeStruct((1, WIDTH), jnp.float32)
    two = jax.ShapeDtypeStruct((2, WIDTH), jnp.float32)
    return call(stage_kernel, "stage", [row, two, edge, edge], [VMEM, SMEM, SMEM, VMEM, VMEM])(*arrays)


def cell_sum_kernel(block, feat, send_a, send_b):
    cell = lax.broadcasted_iota(jnp.int32, (256, 128), 0).astype(jnp.float32)
    total = jnp.zeros((256, 128), jnp.float32)
    ids = jnp.sum(block[:, :, 1024:1152].astype(jnp.float32).reshape(16, 8, 2, 128), axis=1)
    for step in range(4):
        picks = []
        rows = []
        for part in range(4 * step, 4 * step + 4):
            wide = jnp.broadcast_to(ids[part, 0:1], (256, 128))
            picks.append(jnp.where(wide == cell, 1.0, 0.0).astype(jnp.bfloat16))
            rows += [block[8 * part : 8 * part + 8, :, 128 * k : 128 * k + 128].reshape(16, 128) for k in range(8)]
        total = total + dot(jnp.concatenate(picks, axis=1), jnp.concatenate(rows, axis=0))
    total = rounded(total).reshape(16, 16, 128)
    feat[...] = total.astype(jnp.bfloat16)
    even = lax.rem(lax.axis_index("rad"), 2) == 0
    low = total[:, :EDGE]
    high = total[:, EDGE:]
    send_a[...] = jnp.where(even, high, low).astype(jnp.bfloat16)
    send_b[...] = jnp.where(even, low, high).astype(jnp.bfloat16)


def cell_sums(arrived):
    return call(
        cell_sum_kernel,
        "cell_sums",
        [(16, 16, 128), (16, EDGE, 128), (16, EDGE, 128)],
        [VMEM],
    )(arrived)


def widened(own, got_a, got_b):
    even = lax.rem(lax.axis_index("rad"), 2) == 0
    a = got_a[...].astype(jnp.float32)
    b = got_b[...].astype(jnp.float32)
    from_a = (lax.broadcasted_iota(jnp.int32, a.shape, 1) < HALO) == even
    parts = [own[...].astype(jnp.float32), jnp.where(from_a, a, b), jnp.where(from_a, b, a)]
    return jnp.concatenate(parts, axis=1)


def send_halves(x, to_a, to_b):
    even = lax.rem(lax.axis_index("az"), 2) == 0
    to_a[...] = jnp.where(even, x[EDGE:], x[:EDGE]).astype(jnp.bfloat16)
    to_b[...] = jnp.where(even, x[:EDGE], x[EDGE:]).astype(jnp.bfloat16)


def widen_kernel(token, own, got_a, got_b, wide, to_a, to_b):
    x = widened(own, got_a, got_b)
    wide[...] = x.astype(jnp.bfloat16)
    send_halves(x, to_a, to_b)


def widen(*arrays):
    return call(widen_kernel, "widen", [(16, 32, WIDTH)] + [(EDGE, 32, WIDTH)] * 2, [VMEM] * 4)(*arrays)


def streamed(feat, hid, pitch, w_map):
    x = dot(feat.reshape(-1, 128).astype(jnp.bfloat16), w_map[...])
    return rounded(hid.reshape(-1, WIDTH) + x + pitch[...]).reshape(hid.shape)


def band_kernel(feat, feat_b, feat_a, hid, pitch, w_map, stream, to_a, to_b):
    x = widened(feat, feat_a, feat_b)
    send_halves(x, to_a, to_b)
    stream[...] = streamed(x, hid[...].astype(jnp.float32), pitch, w_map).astype(jnp.bfloat16)


def band(*arrays):
    return call(band_kernel, "band", [(16, 32, WIDTH)] + [(EDGE, 32, 128)] * 2, [VMEM] * 6)(*arrays)


def project(w, layer, block, rows, block_ones, target, at, scale=None, plain=False):
    x = dot(rows, w[layer, :, block * 256 : block * 256 + 256])
    lanes = slice(block % 2 * 256, block % 2 * 256 + 256)
    yield
    if not plain:
        x = rounded(x)
        squares = dot((x * x).astype(jnp.bfloat16), block_ones[...])
        yield
        x = x * lax.rsqrt(squares + 1e-06)
    if scale is not None:
        x = x * scale[layer : layer + 1, lanes]
    target[at : at + x.shape[0], lanes] = x.astype(jnp.bfloat16)


def project_all(w, layer, wide, narrow, block_ones, scale, queries, q_at, keys, values, at):
    parts = [project(w, layer, block, wide, block_ones, keys, at) for block in (2, 3)]
    parts += [project(w, layer, block, narrow, block_ones, queries, q_at, scale) for block in (0, 1)]
    return parts + [project(w, layer, block, wide, block_ones, values, at, plain=True) for block in (4, 5)]


def query_lanes(table):
    r = lax.axis_index("rad")
    lane = lax.broadcasted_iota(jnp.int32, (1, 128), 1)
    ends = ((lane == 48) & (r == 0)) | ((lane == 49) & (r == lax.axis_size("rad") - 1))
    return table + jnp.where(ends, 1.0, 0.0).astype(jnp.bfloat16)


def attend(queries, query_aug, keys, key_aug, values, att):
    n = query_aug.shape[0]
    lane = lax.broadcasted_iota(jnp.int32, (1, 128), 1)
    low = jnp.where(lane < 64, 1.0, 0.0).astype(jnp.bfloat16)
    high = jnp.where(lane < 64, 0.0, 1.0).astype(jnp.bfloat16)
    half = lax.broadcasted_iota(jnp.int32, (n, 128), 1) < 64
    one = jnp.ones((key_aug.shape[0], 128), jnp.bfloat16)

    def pair_of_heads(pair):
        lanes = slice(pair * 128, pair * 128 + 128)

        def rows(parts):
            return jnp.concatenate([ref[at : at + count, lanes] for ref, at, count in parts], axis=0)

        q = rows(queries)
        q = jnp.concatenate(
            [jnp.concatenate([q * low, query_aug], axis=1), jnp.concatenate([q * high, query_aug], axis=1)], axis=0
        )
        k = jnp.concatenate([rows(keys), key_aug], axis=1)
        score = lax.dot_general(q, k, (((1,), (1,)), ((), ())), preferred_element_type=jnp.float32)
        yield
        got = dot(jnp.exp2(score).astype(jnp.bfloat16), jnp.concatenate([rows(values), one], axis=1))
        yield
        top = jnp.where(half, got[:n, :128], got[n:, :128])
        total = jnp.where(half, got[:n, 128:], got[n:, 128:])
        att[0:n, lanes] = (top / total).astype(jnp.bfloat16)

    return [pair_of_heads(pair) for pair in range(HEADS // 2)]


def columns(x, at, count, width):
    return x[at : at + count, :width].reshape(count * width, WIDTH)


def inner_kernel(
    band_stream, scale, gains, w_qkv, w_out, block_ones, q_aug, k_aug,
    queries, keys, values, stream, queries_1, keys_1, values_1, att,
):
    x = band_stream[...].astype(jnp.float32)
    normed = norm_rows(x.reshape(512, WIDTH), gains[0:1, :])
    narrow = columns(normed.reshape(16, 32, WIDTH), 0, 16, 24).astype(jnp.bfloat16)
    wide = normed.astype(jnp.bfloat16)
    interleave(project_all(w_qkv, 0, wide, narrow, block_ones, scale, queries, 0, keys, values, 0), 2)
    pairs = attend(
        [(queries, 96, 192)], query_lanes(q_aug[192:384]), [(keys, 0, 512)], k_aug[256:768], [(values, 0, 512)], att
    )
    interleave(pairs, 2)
    x = rounded(columns(x, 4, 8, 24) + dot(att[...], w_out[0]))
    stream[...] = x.astype(jnp.bfloat16)
    normed = norm_rows(x, gains[1:2, :])
    narrow = columns(normed.reshape(8, 24, WIDTH), 0, 8, 16).astype(jnp.bfloat16)
    wide = normed.astype(jnp.bfloat16)
    interleave(project_all(w_qkv, 1, wide, narrow, block_ones, scale, queries_1, 0, keys_1, values_1, 0), 2)


def inner(*arrays):
    outs = [(384, WIDTH), (512, WIDTH), (512, WIDTH), (192, WIDTH), (128, WIDTH), (192, WIDTH), (192, WIDTH)]
    scratch = [pltpu.VMEM((192, WIDTH), jnp.bfloat16)]
    return call(inner_kernel, "inner", outs, [VMEM] * 8, scratch=scratch, mib=14)(*arrays)


def outer_kernel(
    feat_b, feat_a, hid_b, hid_a, band_stream, pitch, w_map, scale, gains, w_qkv, w_out, last_gain, block_ones, q_aug, k_aug, q_aug_1, k_aug_1,
    q_mid, k_mid, v_mid, stream_mid, q1_mid, k1_mid, v1_mid,
    out, q_end, k_end, v_end, q1_end, k1_end, v1_end, att_0, att_1,
):
    att = (att_0, att_1)
    even = lax.rem(lax.axis_index("az"), 2) == 0

    def low_high(from_a, from_b):
        a = from_a[...].astype(jnp.float32)
        b = from_b[...].astype(jnp.float32)
        return jnp.concatenate([jnp.where(even, b, a), jnp.where(even, a, b)], axis=0)

    x = streamed(low_high(feat_a, feat_b), low_high(hid_a, hid_b), pitch, w_map)
    normed = norm_rows(x.reshape(512, WIDTH), gains[0:1, :])
    narrow = columns(normed.reshape(16, 32, WIDTH), 4, 8, 24).astype(jnp.bfloat16)
    wide = normed.astype(jnp.bfloat16)
    interleave(project_all(w_qkv, 0, wide, narrow, block_ones, scale, q_end, 0, k_end, v_end, 0), 2)
    pairs = []
    for part in range(2):
        if part == 0:
            q = [(q_end, 0, 96), (q_mid, 0, 96)]
            k, v = [[(end, 0, 256), (mid, 0, 256)] for end, mid in ((k_end, k_mid), (v_end, v_mid))]
        else:
            q = [(q_mid, 288, 96), (q_end, 96, 96)]
            k, v = [[(mid, 256, 256), (end, 256, 256)] for end, mid in ((k_end, k_mid), (v_end, v_mid))]
        q_lanes = query_lanes(q_aug[384 * part : 384 * part + 192])
        pairs.append(attend(q, q_lanes, k, k_aug[512 * part : 512 * part + 512], v, att[part]))
    kept = [None, None]

    def finish(part):
        at = 4 * (1 - part)
        ours = band_stream[12 * part : 12 * part + 4].astype(jnp.float32)
        before = [columns(x, 4 + 4 * part, 4, 24), columns(ours, 0, 4, 24)]
        y = dot(att[part][...], w_out[0])
        yield
        y = rounded(jnp.concatenate(before if part == 0 else before[::-1], axis=0) + y)
        normed = norm_rows(y, gains[1:2, :])
        narrow = columns(normed.reshape(8, 24, WIDTH), at, 4, 16).astype(jnp.bfloat16)
        kept[part] = columns(y.reshape(8, 24, WIDTH), at, 4, 16)
        yield
        wide = normed.astype(jnp.bfloat16)
        yield from one_by_one(
            *project_all(
                w_qkv, 1, wide, narrow, block_ones, scale, q1_end, 64 * part, k1_end, v1_end, 192 * part
            )
        )

    interleave(pairs[0], 2)
    interleave([one_by_one(*pairs[1]), finish(0)], 2)
    middle = stream_mid[...].astype(jnp.float32).reshape(8, 24, WIDTH)
    pairs = []
    for part in range(2):
        if part == 0:
            q = [(q1_end, 0, 64), (q1_mid, 0, 64)]
            k, v = [[(end, 0, 192), (mid, 0, 192)] for end, mid in ((k1_end, k1_mid), (v1_end, v1_mid))]
        else:
            q = [(q1_mid, 64, 64), (q1_end, 64, 64)]
            k, v = [[(mid, 0, 192), (end, 192, 192)] for end, mid in ((k1_end, k1_mid), (v1_end, v1_mid))]
        q_lanes = query_lanes(q_aug_1[128 * part : 128 * part + 128])
        pairs.append(attend(q, q_lanes, k, k_aug_1[192 * part : 192 * part + 384], v, att[part]))

    def end(part):
        before = [columns(middle, 4 * part, 4, 16), kept[part]]
        y = dot(att[part][0:128], w_out[1])
        yield
        y = rounded(jnp.concatenate(before if part else before[::-1], axis=0) + y)
        latent = norm_rows(y, last_gain[...])
        out[8 * part : 8 * part + 8] = latent.reshape(8, 16, WIDTH).astype(jnp.bfloat16)

    interleave([finish(1), one_by_one(*pairs[0])], 2)
    interleave([one_by_one(*pairs[1]), end(0)], 2)
    interleave([end(1)], 1)


def outer(*arrays):
    scratch = [192, 512, 512, 128, 384, 384, 192, 192]
    return call(
        outer_kernel,
        "outer",
        [(16, 16, WIDTH)],
        [VMEM] * 24,
        scratch=[pltpu.VMEM((rows, WIDTH), jnp.bfloat16) for rows in scratch],
        mib=14,
    )(*arrays)[0]


def swap(x, axis, shift):
    count = lax.axis_size(axis)
    pairs = [(i, ((i + shift) ^ 1) - shift) for i in range(count)]
    if axis == "az":
        pairs = [(i, j % count) for i, j in pairs]
    return lax.ppermute(x, axis, [(i, j) for i, j in pairs if 0 <= j < count])


def per_device(
    hidden_site_vector,
    mesh_portion_descriptors,
    mesh_entry_site,
    mesh_portion_tally,
    incline_grid_position,
    incline_vector_lookup,
    mesh_mapping_matrix,
    prefocus_rescale_factor,
    probe_lock_payload_matrix,
    sharpness_scale,
    final_mapping_matrix,
    terminal_rescale_factor,
):
    packed, token = pack(
        mesh_portion_descriptors.reshape(128, 8, 2, 128), mesh_entry_site.reshape(16, 128), mesh_portion_tally
    )
    arrived = lax.all_to_all(packed, ("az", "rad"), split_axis=0, concat_axis=0, tiled=True)

    hidden = hidden_site_vector[0]
    block_ones = jnp.asarray(np.kron(np.eye(4), np.ones((64, 64))), jnp.bfloat16)
    pitch, scale, to_a, to_b = stage(
        token, incline_grid_position, sharpness_scale, incline_vector_lookup, hidden
    )
    hid_a, hid_b = swap(to_a, "rad", 0), swap(to_b, "rad", 1)

    feat, to_a, to_b = cell_sums(arrived)
    feat_a, feat_b = swap(to_a, "rad", 0), swap(to_b, "rad", 1)
    hid, to_a, to_b = widen(feat, hidden, hid_a, hid_b)
    hid_b, hid_a = swap(to_b, "az", 1), swap(to_a, "az", 0)
    stream, to_a, to_b = band(feat, feat_b, feat_a, hid, pitch, mesh_mapping_matrix)
    feat_b, feat_a = swap(to_b, "az", 1), swap(to_a, "az", 0)
    q_aug, k_aug, q_aug_1, k_aug_1 = window_tables()
    weights = (scale, prefocus_rescale_factor, probe_lock_payload_matrix, final_mapping_matrix)
    middle = inner(stream, *weights, block_ones, q_aug, k_aug)
    out = outer(
        feat_b, feat_a, hid_b, hid_a, stream, pitch, mesh_mapping_matrix, *weights, terminal_rescale_factor[None, :],
        block_ones, q_aug, k_aug, q_aug_1, k_aug_1, *middle,
    )
    return out[None]


def solution(mesh):
    rows = P(("az", "rad"), None)
    in_specs = (P(None, "az", "rad", None), rows, P(("az", "rad")), rows) + (P(),) * 8
    return jax.shard_map(
        per_device,
        mesh=mesh,
        in_specs=in_specs,
        out_specs=P(None, "az", "rad", None),
        check_vma=False,
    )
```

```python
import jax
import jax.numpy as jnp
import numpy as np
from jax import lax
from jax.experimental import pallas as pl
from jax.experimental.pallas import tpu as pltpu
from jax.sharding import PartitionSpec as P

HALO = 4
HEADS = 8
WIDTH = 512
EDGE = 2 * HALO
DEAD = 256
NEG = -1024.0
LOG2E = 1.4426950408889634
COLUMN_J = np.array(
    list(range(8, 24)) + list(range(24, 28)) + list(range(4, 8)) + list(range(0, 4)) + list(range(28, 32))
)
SMEM = pl.BlockSpec(memory_space=pltpu.SMEM)
VMEM = pl.BlockSpec(memory_space=pltpu.VMEM)
HBM = pl.BlockSpec(memory_space=pltpu.HBM)


def window_tables():
    i = np.arange(32)
    key = np.zeros((32, 32, 128), np.float32)
    query = np.zeros((24, 24, 128), np.float32)
    for d in range(24):
        key[:, :, d] = np.where(np.abs(COLUMN_J - COLUMN_J[d]) > HALO, NEG, 0.0)[None, :]
        key[:, :, 24 + d] = np.where(np.abs(i - (d + HALO)) > HALO, NEG, 0.0)[:, None]
        query[:, d, d] = 1.0
        query[d, :, 24 + d] = 1.0
    key[:, :, 48] = np.where(COLUMN_J < 8, NEG, 0.0)[None, :]
    key[:, :, 49] = np.where(COLUMN_J >= 24, NEG, 0.0)[None, :]
    tables = (
        query.reshape(576, 128),
        key.reshape(1024, 128),
        query[4:20, :16].reshape(256, 128),
        key[4:28, :24].reshape(576, 128),
    )
    return [jnp.asarray(t, jnp.bfloat16) for t in tables]


def dot(a, b):
    return jnp.dot(a, b, preferred_element_type=jnp.float32)


def rounded(x):
    return x.astype(jnp.bfloat16).astype(jnp.float32)


def norm_rows(x, gain):
    return x * lax.rsqrt(jnp.mean(x * x, -1, keepdims=True) + 1e-05) * gain


def shape_of(x):
    return x if isinstance(x, jax.ShapeDtypeStruct) else jax.ShapeDtypeStruct(x, jnp.bfloat16)


COST = {"pack": 1.5, "stage": 1, "cell_sums": 2, "band": 1, "widen": 1, "inner": 4, "outer": 8}


def call(kernel, name, outs, in_specs, out_specs=None, scratch=(), mib=8):
    return pl.pallas_call(
        kernel,
        out_shape=[shape_of(x) for x in outs],
        in_specs=in_specs,
        out_specs=out_specs or [VMEM] * len(outs),
        scratch_shapes=scratch,
        compiler_params=pltpu.CompilerParams(vmem_limit_bytes=mib << 20),
        name=name,
        cost_estimate=pl.CostEstimate(
            flops=int(COST[name] * 1e9), bytes_accessed=int(COST[name] * 3e6), transcendentals=0
        ),
    )


def interleave(tasks, depth):
    waiting = list(tasks)
    active = []
    while waiting or active:
        if waiting and len(active) < depth:
            active.append(waiting.pop(0))
        for task in list(active):
            if next(task, True):
                active.remove(task)


def one_by_one(*tasks):
    for task in tasks:
        yield from task


def pack_kernel(rows, cells, tally, packed, block, cells_here, tally_here, sems, out_sems):
    ids_load = pltpu.make_async_copy(cells, cells_here, sems.at[8])
    tally_load = pltpu.make_async_copy(tally, tally_here, sems.at[9])
    ids_load.start()
    tally_load.start()
    loads = [
        pltpu.make_async_copy(rows.at[:, k], block.at[:, :, pl.ds(128 * k, 128)], sems.at[k]) for k in range(8)
    ]
    for load in loads:
        load.start()
    t = lax.broadcasted_iota(jnp.int32, (128, 128), 0)
    lane = lax.broadcasted_iota(jnp.int32, (128, 128), 1)
    mine = t % 8 == lane // 16
    slot = lane % 16
    pick = jnp.where(mine, 1.0, 0.0).astype(jnp.bfloat16)
    r = lax.axis_index("rad")
    order = (lane // 16 == t % 16 // 2) & (lane % 16 == 2 * r + t % 2)
    order = jnp.where(order, 1.0, 0.0).astype(jnp.bfloat16)
    ids_load.wait()
    tally_load.wait()
    here = lax.broadcasted_iota(jnp.int32, (16, 128), 1) // 8 == lax.broadcasted_iota(jnp.int32, (16, 128), 0)
    spread = jnp.where(here, tally_here[...].astype(jnp.float32), 0.0).astype(jnp.bfloat16)
    live = slot[:16].astype(jnp.float32) < dot(spread, pick)
    ids = jnp.where(live, cells_here[...].astype(jnp.float32), float(DEAD))
    ids = jnp.broadcast_to(ids[:, None, :], (16, 8, 128)).reshape(128, 128)
    ids = dot(jnp.where(mine, ids, 0.0).astype(jnp.bfloat16), order)
    for load in loads:
        load.wait()
    stores = [pltpu.make_async_copy(block.at[:, :, 0:1024], packed.at[:, :, 0:1024], out_sems.at[0])]
    stores[0].start()
    for at in range(128):
        block[at, :, 1024:1152] = jnp.broadcast_to(ids[at : at + 1], (2, 128)).astype(jnp.bfloat16)
    stores.append(pltpu.make_async_copy(block.at[:, :, 1024:1152], packed.at[:, :, 1024:1152], out_sems.at[1]))
    stores[1].start()
    for store in stores:
        store.wait()


def pack(rows, cells, tally):
    return call(
        pack_kernel,
        "pack",
        [(128, 2, 1152)],
        [HBM] * 3,
        [HBM],
        [
            pltpu.VMEM((128, 2, 1152), jnp.bfloat16),
            pltpu.VMEM((16, 128), jnp.int32),
            pltpu.VMEM((1, 128), jnp.int32),
            pltpu.SemaphoreType.DMA((10,)),
            pltpu.SemaphoreType.DMA((2,)),
        ],
        mib=60,
    )(rows, cells, tally)[0]


def stage_kernel(packed, pitch_at, sharp, lookup, hidden, pitch, scale, send_a, send_b):
    rows = lax.broadcasted_iota(jnp.int32, (64, 1), 0)
    pitch[...] = jnp.sum(
        jnp.where(rows == pitch_at[0], lookup[...].astype(jnp.float32), 0.0), axis=0, keepdims=True
    )
    head = lax.broadcasted_iota(jnp.int32, (1, WIDTH), 1) // 64
    for layer in range(2):
        line = jnp.zeros((1, WIDTH), jnp.float32)
        for h in range(HEADS):
            line = jnp.where(head == h, sharp[layer, h] * LOG2E, line)
        scale[layer : layer + 1] = line
    even = lax.rem(lax.axis_index("rad"), 2) == 0
    low = hidden[:, :EDGE].astype(jnp.float32)
    high = hidden[:, EDGE:].astype(jnp.float32)
    send_a[...] = jnp.where(even, high, low).astype(jnp.bfloat16)
    send_b[...] = jnp.where(even, low, high).astype(jnp.bfloat16)


def stage(*arrays):
    edge = (16, EDGE, WIDTH)
    row = jax.ShapeDtypeStruct((1, WIDTH), jnp.float32)
    two = jax.ShapeDtypeStruct((2, WIDTH), jnp.float32)
    return call(stage_kernel, "stage", [row, two, edge, edge], [HBM, SMEM, SMEM, VMEM, VMEM])(*arrays)


def cell_sum_kernel(block, feat, send_a, send_b):
    cell = lax.broadcasted_iota(jnp.int32, (256, 128), 0).astype(jnp.float32)
    total = jnp.zeros((256, 128), jnp.float32)
    ids = jnp.sum(block[:, :, 1024:1152].astype(jnp.float32).reshape(16, 8, 2, 128), axis=1)
    for step in range(4):
        picks = []
        rows = []
        for part in range(4 * step, 4 * step + 4):
            wide = jnp.broadcast_to(ids[part, 0:1], (256, 128))
            picks.append(jnp.where(wide == cell, 1.0, 0.0).astype(jnp.bfloat16))
            rows += [block[8 * part : 8 * part + 8, :, 128 * k : 128 * k + 128].reshape(16, 128) for k in range(8)]
        total = total + dot(jnp.concatenate(picks, axis=1), jnp.concatenate(rows, axis=0))
    total = rounded(total).reshape(16, 16, 128)
    feat[...] = total.astype(jnp.bfloat16)
    even = lax.rem(lax.axis_index("rad"), 2) == 0
    low = total[:, :EDGE]
    high = total[:, EDGE:]
    send_a[...] = jnp.where(even, high, low).astype(jnp.bfloat16)
    send_b[...] = jnp.where(even, low, high).astype(jnp.bfloat16)


def cell_sums(arrived):
    return call(
        cell_sum_kernel,
        "cell_sums",
        [(16, 16, 128), (16, EDGE, 128), (16, EDGE, 128)],
        [VMEM],
    )(arrived)


def widened(own, got_a, got_b):
    even = lax.rem(lax.axis_index("rad"), 2) == 0
    a = got_a[...].astype(jnp.float32)
    b = got_b[...].astype(jnp.float32)
    from_a = (lax.broadcasted_iota(jnp.int32, a.shape, 1) < HALO) == even
    parts = [own[...].astype(jnp.float32), jnp.where(from_a, a, b), jnp.where(from_a, b, a)]
    return jnp.concatenate(parts, axis=1)


def send_halves(x, to_a, to_b):
    even = lax.rem(lax.axis_index("az"), 2) == 0
    to_a[...] = jnp.where(even, x[EDGE:], x[:EDGE]).astype(jnp.bfloat16)
    to_b[...] = jnp.where(even, x[:EDGE], x[EDGE:]).astype(jnp.bfloat16)


def widen_kernel(token, own, got_a, got_b, wide, to_a, to_b):
    x = widened(own, got_a, got_b)
    wide[...] = x.astype(jnp.bfloat16)
    send_halves(x, to_a, to_b)


def widen(*arrays):
    return call(widen_kernel, "widen", [(16, 32, WIDTH)] + [(EDGE, 32, WIDTH)] * 2, [VMEM] * 4)(*arrays)


def streamed(feat, hid, pitch, w_map):
    x = dot(feat.reshape(-1, 128).astype(jnp.bfloat16), w_map[...])
    return rounded(hid.reshape(-1, WIDTH) + x + pitch[...]).reshape(hid.shape)


def band_kernel(feat, feat_b, feat_a, hid, pitch, w_map, stream, to_a, to_b):
    x = widened(feat, feat_a, feat_b)
    send_halves(x, to_a, to_b)
    stream[...] = streamed(x, hid[...].astype(jnp.float32), pitch, w_map).astype(jnp.bfloat16)


def band(*arrays):
    return call(band_kernel, "band", [(16, 32, WIDTH)] + [(EDGE, 32, 128)] * 2, [VMEM] * 6)(*arrays)


def project(w, layer, block, rows, block_ones, target, at, scale=None, plain=False):
    x = dot(rows, w[layer, :, block * 256 : block * 256 + 256])
    lanes = slice(block % 2 * 256, block % 2 * 256 + 256)
    yield
    if not plain:
        x = rounded(x)
        squares = dot((x * x).astype(jnp.bfloat16), block_ones[...])
        yield
        x = x * lax.rsqrt(squares + 1e-06)
    if scale is not None:
        x = x * scale[layer : layer + 1, lanes]
    target[at : at + x.shape[0], lanes] = x.astype(jnp.bfloat16)


def project_all(w, layer, wide, narrow, block_ones, scale, queries, q_at, keys, values, at):
    parts = [project(w, layer, block, wide, block_ones, keys, at) for block in (2, 3)]
    parts += [project(w, layer, block, narrow, block_ones, queries, q_at, scale) for block in (0, 1)]
    return parts + [project(w, layer, block, wide, block_ones, values, at, plain=True) for block in (4, 5)]


def query_lanes(table):
    r = lax.axis_index("rad")
    lane = lax.broadcasted_iota(jnp.int32, (1, 128), 1)
    ends = ((lane == 48) & (r == 0)) | ((lane == 49) & (r == lax.axis_size("rad") - 1))
    return table + jnp.where(ends, 1.0, 0.0).astype(jnp.bfloat16)


def attend(queries, query_aug, keys, key_aug, values, att):
    n = query_aug.shape[0]
    lane = lax.broadcasted_iota(jnp.int32, (1, 128), 1)
    low = jnp.where(lane < 64, 1.0, 0.0).astype(jnp.bfloat16)
    high = jnp.where(lane < 64, 0.0, 1.0).astype(jnp.bfloat16)
    half = lax.broadcasted_iota(jnp.int32, (n, 128), 1) < 64
    one = jnp.ones((key_aug.shape[0], 128), jnp.bfloat16)

    def pair_of_heads(pair):
        lanes = slice(pair * 128, pair * 128 + 128)

        def rows(parts):
            return jnp.concatenate([ref[at : at + count, lanes] for ref, at, count in parts], axis=0)

        q = rows(queries)
        q = jnp.concatenate(
            [jnp.concatenate([q * low, query_aug], axis=1), jnp.concatenate([q * high, query_aug], axis=1)], axis=0
        )
        k = jnp.concatenate([rows(keys), key_aug], axis=1)
        score = lax.dot_general(q, k, (((1,), (1,)), ((), ())), preferred_element_type=jnp.float32)
        yield
        got = dot(jnp.exp2(score).astype(jnp.bfloat16), jnp.concatenate([rows(values), one], axis=1))
        yield
        top = jnp.where(half, got[:n, :128], got[n:, :128])
        total = jnp.where(half, got[:n, 128:], got[n:, 128:])
        att[0:n, lanes] = (top / total).astype(jnp.bfloat16)

    return [pair_of_heads(pair) for pair in range(HEADS // 2)]


def columns(x, at, count, width):
    return x[at : at + count, :width].reshape(count * width, WIDTH)


def inner_kernel(
    band_stream, scale, gains, w_qkv, w_out, block_ones, q_aug, k_aug,
    queries, keys, values, stream, queries_1, keys_1, values_1, att,
):
    x = band_stream[...].astype(jnp.float32)
    normed = norm_rows(x.reshape(512, WIDTH), gains[0:1, :])
    narrow = columns(normed.reshape(16, 32, WIDTH), 0, 16, 24).astype(jnp.bfloat16)
    wide = normed.astype(jnp.bfloat16)
    interleave(project_all(w_qkv, 0, wide, narrow, block_ones, scale, queries, 0, keys, values, 0), 2)
    pairs = attend(
        [(queries, 96, 192)], query_lanes(q_aug[192:384]), [(keys, 0, 512)], k_aug[256:768], [(values, 0, 512)], att
    )
    interleave(pairs, 2)
    x = rounded(columns(x, 4, 8, 24) + dot(att[...], w_out[0]))
    stream[...] = x.astype(jnp.bfloat16)
    normed = norm_rows(x, gains[1:2, :])
    narrow = columns(normed.reshape(8, 24, WIDTH), 0, 8, 16).astype(jnp.bfloat16)
    wide = normed.astype(jnp.bfloat16)
    interleave(project_all(w_qkv, 1, wide, narrow, block_ones, scale, queries_1, 0, keys_1, values_1, 0), 2)


def inner(*arrays):
    outs = [(384, WIDTH), (512, WIDTH), (512, WIDTH), (192, WIDTH), (128, WIDTH), (192, WIDTH), (192, WIDTH)]
    scratch = [pltpu.VMEM((192, WIDTH), jnp.bfloat16)]
    return call(inner_kernel, "inner", outs, [VMEM] * 8, scratch=scratch, mib=14)(*arrays)


def outer_kernel(
    feat_b, feat_a, hid_b, hid_a, band_stream, pitch, w_map, scale, gains, w_qkv, w_out, last_gain, block_ones, q_aug, k_aug, q_aug_1, k_aug_1,
    q_mid, k_mid, v_mid, stream_mid, q1_mid, k1_mid, v1_mid,
    out, q_end, k_end, v_end, q1_end, k1_end, v1_end, att_0, att_1,
):
    att = (att_0, att_1)
    even = lax.rem(lax.axis_index("az"), 2) == 0

    def low_high(from_a, from_b):
        a, b = from_a[...], from_b[...]
        return jnp.concatenate([jnp.where(even, b, a), jnp.where(even, a, b)], axis=0)

    x = streamed(low_high(feat_a, feat_b), low_high(hid_a, hid_b).astype(jnp.float32), pitch, w_map)
    normed = norm_rows(x.reshape(512, WIDTH), gains[0:1, :])
    narrow = columns(normed.reshape(16, 32, WIDTH), 4, 8, 24).astype(jnp.bfloat16)
    wide = normed.astype(jnp.bfloat16)
    interleave(project_all(w_qkv, 0, wide, narrow, block_ones, scale, q_end, 0, k_end, v_end, 0), 2)
    pairs = []
    for part in range(2):
        if part == 0:
            q = [(q_end, 0, 96), (q_mid, 0, 96)]
            k, v = [[(end, 0, 256), (mid, 0, 256)] for end, mid in ((k_end, k_mid), (v_end, v_mid))]
        else:
            q = [(q_mid, 288, 96), (q_end, 96, 96)]
            k, v = [[(mid, 256, 256), (end, 256, 256)] for end, mid in ((k_end, k_mid), (v_end, v_mid))]
        q_lanes = query_lanes(q_aug[384 * part : 384 * part + 192])
        pairs.append(attend(q, q_lanes, k, k_aug[512 * part : 512 * part + 512], v, att[part]))
    kept = [None, None]

    def finish(part):
        at = 4 * (1 - part)
        ours = band_stream[12 * part : 12 * part + 4].astype(jnp.float32)
        before = [columns(x, 4 + 4 * part, 4, 24), columns(ours, 0, 4, 24)]
        y = dot(att[part][...], w_out[0])
        yield
        y = rounded(jnp.concatenate(before if part == 0 else before[::-1], axis=0) + y)
        normed = norm_rows(y, gains[1:2, :])
        narrow = columns(normed.reshape(8, 24, WIDTH), at, 4, 16).astype(jnp.bfloat16)
        kept[part] = columns(y.reshape(8, 24, WIDTH), at, 4, 16)
        yield
        wide = normed.astype(jnp.bfloat16)
        yield from one_by_one(
            *project_all(
                w_qkv, 1, wide, narrow, block_ones, scale, q1_end, 64 * part, k1_end, v1_end, 192 * part
            )
        )

    interleave(pairs[0], 2)
    interleave([one_by_one(*pairs[1]), finish(0)], 2)
    middle = stream_mid[...].astype(jnp.float32).reshape(8, 24, WIDTH)
    pairs = []
    for part in range(2):
        if part == 0:
            q = [(q1_end, 0, 64), (q1_mid, 0, 64)]
            k, v = [[(end, 0, 192), (mid, 0, 192)] for end, mid in ((k1_end, k1_mid), (v1_end, v1_mid))]
        else:
            q = [(q1_mid, 64, 64), (q1_end, 64, 64)]
            k, v = [[(mid, 0, 192), (end, 192, 192)] for end, mid in ((k1_end, k1_mid), (v1_end, v1_mid))]
        q_lanes = query_lanes(q_aug_1[128 * part : 128 * part + 128])
        pairs.append(attend(q, q_lanes, k, k_aug_1[192 * part : 192 * part + 384], v, att[part]))

    def end(part):
        before = [columns(middle, 4 * part, 4, 16), kept[part]]
        y = dot(att[part][0:128], w_out[1])
        yield
        y = rounded(jnp.concatenate(before if part else before[::-1], axis=0) + y)
        latent = norm_rows(y, last_gain[...])
        out[8 * part : 8 * part + 8] = latent.reshape(8, 16, WIDTH).astype(jnp.bfloat16)

    interleave([finish(1), one_by_one(*pairs[0])], 2)
    interleave([one_by_one(*pairs[1]), end(0)], 2)
    interleave([end(1)], 1)


def outer(*arrays):
    scratch = [192, 512, 512, 128, 384, 384, 192, 192]
    return call(
        outer_kernel,
        "outer",
        [(16, 16, WIDTH)],
        [VMEM] * 24,
        scratch=[pltpu.VMEM((rows, WIDTH), jnp.bfloat16) for rows in scratch],
        mib=14,
    )(*arrays)[0]


def swap(x, axis, shift):
    count = lax.axis_size(axis)
    pairs = [(i, ((i + shift) ^ 1) - shift) for i in range(count)]
    if axis == "az":
        pairs = [(i, j % count) for i, j in pairs]
    return lax.ppermute(x, axis, [(i, j) for i, j in pairs if 0 <= j < count])


def per_device(
    hidden_site_vector,
    mesh_portion_descriptors,
    mesh_entry_site,
    mesh_portion_tally,
    incline_grid_position,
    incline_vector_lookup,
    mesh_mapping_matrix,
    prefocus_rescale_factor,
    probe_lock_payload_matrix,
    sharpness_scale,
    final_mapping_matrix,
    terminal_rescale_factor,
):
    packed = pack(
        mesh_portion_descriptors.reshape(128, 8, 2, 128), mesh_entry_site.reshape(16, 128), mesh_portion_tally
    )
    arrived = lax.all_to_all(packed, ("az", "rad"), split_axis=0, concat_axis=0, tiled=True)

    hidden = hidden_site_vector[0]
    block_ones = jnp.asarray(np.kron(np.eye(4), np.ones((64, 64))), jnp.bfloat16)
    pitch, scale, to_a, to_b = stage(
        packed, incline_grid_position, sharpness_scale, incline_vector_lookup, hidden
    )
    hid_a, hid_b = swap(to_a, "rad", 0), swap(to_b, "rad", 1)

    feat, to_a, to_b = cell_sums(arrived)
    feat_a, feat_b = swap(to_a, "rad", 0), swap(to_b, "rad", 1)
    hid, to_a, to_b = widen(feat, hidden, hid_a, hid_b)
    hid_b, hid_a = swap(to_b, "az", 1), swap(to_a, "az", 0)
    stream, to_a, to_b = band(feat, feat_b, feat_a, hid, pitch, mesh_mapping_matrix)
    feat_b, feat_a = swap(to_b, "az", 1), swap(to_a, "az", 0)
    q_aug, k_aug, q_aug_1, k_aug_1 = window_tables()
    weights = (scale, prefocus_rescale_factor, probe_lock_payload_matrix, final_mapping_matrix)
    middle = inner(stream, *weights, block_ones, q_aug, k_aug)
    out = outer(
        feat_b, feat_a, hid_b, hid_a, stream, pitch, mesh_mapping_matrix, *weights, terminal_rescale_factor[None, :],
        block_ones, q_aug, k_aug, q_aug_1, k_aug_1, *middle,
    )
    return out[None]


def solution(mesh):
    rows = P(("az", "rad"), None)
    in_specs = (P(None, "az", "rad", None), rows, P(("az", "rad")), rows) + (P(),) * 8
    return jax.shard_map(
        per_device,
        mesh=mesh,
        in_specs=in_specs,
        out_specs=P(None, "az", "rad", None),
        check_vma=False,
    )
```

```python
import jax
import jax.numpy as jnp
import numpy as np
from jax import lax
from jax.experimental import pallas as pl
from jax.experimental.pallas import tpu as pltpu
from jax.sharding import PartitionSpec as P

HALO = 4
HEADS = 8
WIDTH = 512
EDGE = 2 * HALO
DEAD = 256
NEG = -1024.0
LOG2E = 1.4426950408889634
COLUMN_J = np.array(
    list(range(8, 24)) + list(range(24, 28)) + list(range(4, 8)) + list(range(0, 4)) + list(range(28, 32))
)
SMEM = pl.BlockSpec(memory_space=pltpu.SMEM)
VMEM = pl.BlockSpec(memory_space=pltpu.VMEM)
HBM = pl.BlockSpec(memory_space=pltpu.HBM)


def window_tables():
    i = np.arange(32)
    key = np.zeros((32, 32, 128), np.float32)
    query = np.zeros((24, 24, 128), np.float32)
    for d in range(24):
        key[:, :, d] = np.where(np.abs(COLUMN_J - COLUMN_J[d]) > HALO, NEG, 0.0)[None, :]
        key[:, :, 24 + d] = np.where(np.abs(i - (d + HALO)) > HALO, NEG, 0.0)[:, None]
        query[:, d, d] = 1.0
        query[d, :, 24 + d] = 1.0
    key[:, :, 48] = np.where(COLUMN_J < 8, NEG, 0.0)[None, :]
    key[:, :, 49] = np.where(COLUMN_J >= 24, NEG, 0.0)[None, :]
    tables = (
        query.reshape(576, 128),
        key.reshape(1024, 128),
        query[4:20, :16].reshape(256, 128),
        key[4:28, :24].reshape(576, 128),
    )
    return [jnp.asarray(t, jnp.bfloat16) for t in tables]


def dot(a, b):
    return jnp.dot(a, b, preferred_element_type=jnp.float32)


def rounded(x):
    return x.astype(jnp.bfloat16).astype(jnp.float32)


def norm_rows(x, gain):
    return x * lax.rsqrt(jnp.mean(x * x, -1, keepdims=True) + 1e-05) * gain


def shape_of(x):
    return x if isinstance(x, jax.ShapeDtypeStruct) else jax.ShapeDtypeStruct(x, jnp.bfloat16)


COST = {"pack": 1.5, "stage": 1, "cell_sums": 2, "band": 1, "widen": 1, "inner": 4, "outer": 8}


def call(kernel, name, outs, in_specs, out_specs=None, scratch=(), mib=8):
    return pl.pallas_call(
        kernel,
        out_shape=[shape_of(x) for x in outs],
        in_specs=in_specs,
        out_specs=out_specs or [VMEM] * len(outs),
        scratch_shapes=scratch,
        compiler_params=pltpu.CompilerParams(vmem_limit_bytes=mib << 20),
        name=name,
        cost_estimate=pl.CostEstimate(
            flops=int(COST[name] * 1e9), bytes_accessed=int(COST[name] * 3e6), transcendentals=0
        ),
    )


def interleave(tasks, depth):
    waiting = list(tasks)
    active = []
    while waiting or active:
        if waiting and len(active) < depth:
            active.append(waiting.pop(0))
        for task in list(active):
            if next(task, True):
                active.remove(task)


def one_by_one(*tasks):
    for task in tasks:
        yield from task


def pack_kernel(rows, cells, tally, packed, block, cells_here, tally_here, sems, out_sems):
    ids_load = pltpu.make_async_copy(cells, cells_here, sems.at[8])
    tally_load = pltpu.make_async_copy(tally, tally_here, sems.at[9])
    ids_load.start()
    tally_load.start()
    loads = [
        pltpu.make_async_copy(rows.at[:, k], block.at[:, :, pl.ds(128 * k, 128)], sems.at[k]) for k in range(8)
    ]
    for load in loads:
        load.start()
    t = lax.broadcasted_iota(jnp.int32, (128, 128), 0)
    lane = lax.broadcasted_iota(jnp.int32, (128, 128), 1)
    mine = t % 8 == lane // 16
    slot = lane % 16
    pick = jnp.where(mine, 1.0, 0.0).astype(jnp.bfloat16)
    r = lax.axis_index("rad")
    order = (lane // 16 == t % 16 // 2) & (lane % 16 == 2 * r + t % 2)
    order = jnp.where(order, 1.0, 0.0).astype(jnp.bfloat16)
    ids_load.wait()
    tally_load.wait()
    here = lax.broadcasted_iota(jnp.int32, (16, 128), 1) // 8 == lax.broadcasted_iota(jnp.int32, (16, 128), 0)
    spread = jnp.where(here, tally_here[...].astype(jnp.float32), 0.0).astype(jnp.bfloat16)
    live = slot[:16].astype(jnp.float32) < dot(spread, pick)
    ids = jnp.where(live, cells_here[...].astype(jnp.float32), float(DEAD))
    ids = jnp.broadcast_to(ids[:, None, :], (16, 8, 128)).reshape(128, 128)
    ids = dot(jnp.where(mine, ids, 0.0).astype(jnp.bfloat16), order)
    for load in loads:
        load.wait()
    stores = [pltpu.make_async_copy(block.at[:, :, 0:1024], packed.at[:, :, 0:1024], out_sems.at[0])]
    stores[0].start()
    for at in range(128):
        block[at, :, 1024:1152] = jnp.broadcast_to(ids[at : at + 1], (2, 128)).astype(jnp.bfloat16)
    stores.append(pltpu.make_async_copy(block.at[:, :, 1024:1152], packed.at[:, :, 1024:1152], out_sems.at[1]))
    stores[1].start()
    for store in stores:
        store.wait()


def pack(rows, cells, tally):
    return call(
        pack_kernel,
        "pack",
        [(128, 2, 1152)],
        [HBM] * 3,
        [HBM],
        [
            pltpu.VMEM((128, 2, 1152), jnp.bfloat16),
            pltpu.VMEM((16, 128), jnp.int32),
            pltpu.VMEM((1, 128), jnp.int32),
            pltpu.SemaphoreType.DMA((10,)),
            pltpu.SemaphoreType.DMA((2,)),
        ],
        mib=60,
    )(rows, cells, tally)[0]


def stage_kernel(packed, pitch_at, sharp, lookup, hidden, pitch, scale, send_a, send_b):
    rows = lax.broadcasted_iota(jnp.int32, (64, 1), 0)
    pitch[...] = jnp.sum(
        jnp.where(rows == pitch_at[0], lookup[...].astype(jnp.float32), 0.0), axis=0, keepdims=True
    )
    head = lax.broadcasted_iota(jnp.int32, (1, WIDTH), 1) // 64
    for layer in range(2):
        line = jnp.zeros((1, WIDTH), jnp.float32)
        for h in range(HEADS):
            line = jnp.where(head == h, sharp[layer, h] * LOG2E, line)
        scale[layer : layer + 1] = line
    even = lax.rem(lax.axis_index("rad"), 2) == 0
    low = hidden[:, :EDGE].astype(jnp.float32)
    high = hidden[:, EDGE:].astype(jnp.float32)
    send_a[...] = jnp.where(even, high, low).astype(jnp.bfloat16)
    send_b[...] = jnp.where(even, low, high).astype(jnp.bfloat16)


def stage(*arrays):
    edge = (16, EDGE, WIDTH)
    row = jax.ShapeDtypeStruct((1, WIDTH), jnp.float32)
    two = jax.ShapeDtypeStruct((2, WIDTH), jnp.float32)
    return call(stage_kernel, "stage", [row, two, edge, edge], [HBM, SMEM, SMEM, VMEM, VMEM])(*arrays)


def cell_sum_kernel(block, feat, send_a, send_b):
    cell = lax.broadcasted_iota(jnp.int32, (256, 128), 0).astype(jnp.float32)
    total = jnp.zeros((256, 128), jnp.float32)
    ids = jnp.sum(block[:, :, 1024:1152].astype(jnp.float32).reshape(16, 8, 2, 128), axis=1)
    for step in range(4):
        picks = []
        rows = []
        for part in range(4 * step, 4 * step + 4):
            wide = jnp.broadcast_to(ids[part, 0:1], (256, 128))
            picks.append(jnp.where(wide == cell, 1.0, 0.0).astype(jnp.bfloat16))
            rows += [block[8 * part : 8 * part + 8, :, 128 * k : 128 * k + 128].reshape(16, 128) for k in range(8)]
        total = total + dot(jnp.concatenate(picks, axis=1), jnp.concatenate(rows, axis=0))
    total = rounded(total).reshape(16, 16, 128)
    feat[...] = total.astype(jnp.bfloat16)
    even = lax.rem(lax.axis_index("rad"), 2) == 0
    low = total[:, :EDGE]
    high = total[:, EDGE:]
    send_a[...] = jnp.where(even, high, low).astype(jnp.bfloat16)
    send_b[...] = jnp.where(even, low, high).astype(jnp.bfloat16)


def cell_sums(arrived):
    return call(
        cell_sum_kernel,
        "cell_sums",
        [(16, 16, 128), (16, EDGE, 128), (16, EDGE, 128)],
        [VMEM],
    )(arrived)


def widened(own, got_a, got_b):
    even = lax.rem(lax.axis_index("rad"), 2) == 0
    a = got_a[...].astype(jnp.float32)
    b = got_b[...].astype(jnp.float32)
    from_a = (lax.broadcasted_iota(jnp.int32, a.shape, 1) < HALO) == even
    parts = [own[...].astype(jnp.float32), jnp.where(from_a, a, b), jnp.where(from_a, b, a)]
    return jnp.concatenate(parts, axis=1)


def send_halves(x, to_a, to_b):
    even = lax.rem(lax.axis_index("az"), 2) == 0
    to_a[...] = jnp.where(even, x[EDGE:], x[:EDGE]).astype(jnp.bfloat16)
    to_b[...] = jnp.where(even, x[:EDGE], x[EDGE:]).astype(jnp.bfloat16)


def widen_kernel(token, own, got_a, got_b, wide, to_a, to_b):
    x = widened(own, got_a, got_b)
    wide[...] = x.astype(jnp.bfloat16)
    send_halves(x, to_a, to_b)


def widen(*arrays):
    return call(widen_kernel, "widen", [(16, 32, WIDTH)] + [(EDGE, 32, WIDTH)] * 2, [VMEM] * 4)(*arrays)


def streamed(feat, hid, pitch, w_map):
    x = dot(feat.reshape(-1, 128).astype(jnp.bfloat16), w_map[...])
    return rounded(hid.reshape(-1, WIDTH) + x + pitch[...]).reshape(hid.shape)


def band_kernel(feat, feat_b, feat_a, hid, pitch, w_map, stream, to_a, to_b):
    x = widened(feat, feat_a, feat_b)
    send_halves(x, to_a, to_b)
    stream[...] = streamed(x, hid[...].astype(jnp.float32), pitch, w_map).astype(jnp.bfloat16)


def band(*arrays):
    return call(band_kernel, "band", [(16, 32, WIDTH)] + [(EDGE, 32, 128)] * 2, [VMEM] * 6)(*arrays)


def project(w, layer, block, rows, block_ones, target, at, scale=None, plain=False):
    x = dot(rows, w[layer, :, block * 256 : block * 256 + 256])
    lanes = slice(block % 2 * 256, block % 2 * 256 + 256)
    yield
    if not plain:
        x = rounded(x)
        squares = dot((x * x).astype(jnp.bfloat16), block_ones[...])
        yield
        x = x * lax.rsqrt(squares + 1e-06)
    if scale is not None:
        x = x * scale[layer : layer + 1, lanes]
    target[at : at + x.shape[0], lanes] = x.astype(jnp.bfloat16)


def project_all(w, layer, wide, narrow, block_ones, scale, queries, q_at, keys, values, at):
    parts = [project(w, layer, block, wide, block_ones, keys, at) for block in (2, 3)]
    parts += [project(w, layer, block, narrow, block_ones, queries, q_at, scale) for block in (0, 1)]
    return parts + [project(w, layer, block, wide, block_ones, values, at, plain=True) for block in (4, 5)]


def query_lanes(table):
    r = lax.axis_index("rad")
    lane = lax.broadcasted_iota(jnp.int32, (1, 128), 1)
    ends = ((lane == 48) & (r == 0)) | ((lane == 49) & (r == lax.axis_size("rad") - 1))
    return table + jnp.where(ends, 1.0, 0.0).astype(jnp.bfloat16)


def attend(queries, query_aug, keys, key_aug, values, att, att_at=0):
    n = query_aug.shape[0]
    lane = lax.broadcasted_iota(jnp.int32, (1, 128), 1)
    low = jnp.where(lane < 64, 1.0, 0.0).astype(jnp.bfloat16)
    high = jnp.where(lane < 64, 0.0, 1.0).astype(jnp.bfloat16)
    half = lax.broadcasted_iota(jnp.int32, (n, 128), 1) < 64
    one = jnp.ones((key_aug.shape[0], 128), jnp.bfloat16)

    def pair_of_heads(pair):
        lanes = slice(pair * 128, pair * 128 + 128)

        def rows(parts):
            return jnp.concatenate([ref[at : at + count, lanes] for ref, at, count in parts], axis=0)

        q = rows(queries)
        q = jnp.concatenate(
            [jnp.concatenate([q * low, query_aug], axis=1), jnp.concatenate([q * high, query_aug], axis=1)], axis=0
        )
        k = jnp.concatenate([rows(keys), key_aug], axis=1)
        score = lax.dot_general(q, k, (((1,), (1,)), ((), ())), preferred_element_type=jnp.float32)
        yield
        got = dot(jnp.exp2(score).astype(jnp.bfloat16), jnp.concatenate([rows(values), one], axis=1))
        yield
        top = jnp.where(half, got[:n, :128], got[n:, :128])
        total = jnp.where(half, got[:n, 128:], got[n:, 128:])
        att[att_at : att_at + n, lanes] = (top / total).astype(jnp.bfloat16)

    return [pair_of_heads(pair) for pair in range(HEADS // 2)]


def columns(x, at, count, width):
    return x[at : at + count, :width].reshape(count * width, WIDTH)


def inner_kernel(
    band_stream, scale, gains, w_qkv, w_out, block_ones, q_aug, k_aug,
    queries, keys, values, stream, queries_1, keys_1, values_1, att,
):
    x = band_stream[...].astype(jnp.float32)
    normed = norm_rows(x.reshape(512, WIDTH), gains[0:1, :])
    narrow = columns(normed.reshape(16, 32, WIDTH), 0, 16, 24).astype(jnp.bfloat16)
    wide = normed.astype(jnp.bfloat16)
    interleave(project_all(w_qkv, 0, wide, narrow, block_ones, scale, queries, 0, keys, values, 0), 3)
    pairs = attend(
        [(queries, 96, 192)], query_lanes(q_aug[192:384]), [(keys, 0, 512)], k_aug[256:768], [(values, 0, 512)], att
    )
    interleave(pairs, 2)
    x = rounded(columns(x, 4, 8, 24) + dot(att[...], w_out[0]))
    stream[...] = x.astype(jnp.bfloat16)
    normed = norm_rows(x, gains[1:2, :])
    narrow = columns(normed.reshape(8, 24, WIDTH), 0, 8, 16).astype(jnp.bfloat16)
    wide = normed.astype(jnp.bfloat16)
    interleave(project_all(w_qkv, 1, wide, narrow, block_ones, scale, queries_1, 0, keys_1, values_1, 0), 4)


def inner(*arrays):
    outs = [(384, WIDTH), (512, WIDTH), (512, WIDTH), (192, WIDTH), (128, WIDTH), (192, WIDTH), (192, WIDTH)]
    scratch = [pltpu.VMEM((192, WIDTH), jnp.bfloat16)]
    return call(inner_kernel, "inner", outs, [VMEM] * 8, scratch=scratch, mib=14)(*arrays)


def outer_kernel(
    feat_b, feat_a, hid_b, hid_a, band_stream, pitch, w_map, scale, gains, w_qkv, w_out, last_gain, block_ones, q_aug, k_aug, q_aug_1, k_aug_1,
    q_mid, k_mid, v_mid, stream_mid, q1_mid, k1_mid, v1_mid,
    out, q_end, k_end, v_end, q1_end, k1_end, v1_end, att,
):
    even = lax.rem(lax.axis_index("az"), 2) == 0

    def low_high(from_a, from_b):
        a, b = from_a[...], from_b[...]
        return jnp.concatenate([jnp.where(even, b, a), jnp.where(even, a, b)], axis=0)

    x = streamed(low_high(feat_a, feat_b), low_high(hid_a, hid_b).astype(jnp.float32), pitch, w_map)
    normed = norm_rows(x.reshape(512, WIDTH), gains[0:1, :])
    narrow = columns(normed.reshape(16, 32, WIDTH), 4, 8, 24).astype(jnp.bfloat16)
    wide = normed.astype(jnp.bfloat16)
    interleave(project_all(w_qkv, 0, wide, narrow, block_ones, scale, q_end, 0, k_end, v_end, 0), 3)
    pairs = []
    for part in range(2):
        if part == 0:
            q = [(q_end, 0, 96), (q_mid, 0, 96)]
            k, v = [[(end, 0, 256), (mid, 0, 256)] for end, mid in ((k_end, k_mid), (v_end, v_mid))]
        else:
            q = [(q_mid, 288, 96), (q_end, 96, 96)]
            k, v = [[(mid, 256, 256), (end, 256, 256)] for end, mid in ((k_end, k_mid), (v_end, v_mid))]
        q_lanes = query_lanes(q_aug[384 * part : 384 * part + 192])
        pairs += attend(q, q_lanes, k, k_aug[512 * part : 512 * part + 512], v, att, 192 * part)
    interleave(pairs, 2)
    ours = [columns(band_stream[at : at + 4].astype(jnp.float32), 0, 4, 24) for at in (0, 12)]
    before = [columns(x, 4, 4, 24), *ours, columns(x, 8, 4, 24)]
    y = rounded(jnp.concatenate(before, axis=0) + dot(att[...], w_out[0]))
    normed = norm_rows(y, gains[1:2, :])
    kept = columns(y.reshape(16, 24, WIDTH), 4, 8, 16)
    narrow = columns(normed.reshape(16, 24, WIDTH), 4, 8, 16).astype(jnp.bfloat16)
    wide = normed.astype(jnp.bfloat16)
    interleave(project_all(w_qkv, 1, wide, narrow, block_ones, scale, q1_end, 0, k1_end, v1_end, 0), 4)
    pairs = []
    for part in range(2):
        if part == 0:
            q = [(q1_end, 0, 64), (q1_mid, 0, 64)]
            k, v = [[(end, 0, 192), (mid, 0, 192)] for end, mid in ((k1_end, k1_mid), (v1_end, v1_mid))]
        else:
            q = [(q1_mid, 64, 64), (q1_end, 64, 64)]
            k, v = [[(mid, 0, 192), (end, 192, 192)] for end, mid in ((k1_end, k1_mid), (v1_end, v1_mid))]
        q_lanes = query_lanes(q_aug_1[128 * part : 128 * part + 128])
        pairs += attend(q, q_lanes, k, k_aug_1[192 * part : 192 * part + 384], v, att, 128 * part)
    interleave(pairs, 2)
    middle = columns(stream_mid[...].astype(jnp.float32).reshape(8, 24, WIDTH), 0, 8, 16)
    before = jnp.concatenate([kept[:64], middle, kept[64:]], axis=0)
    y = rounded(before + dot(att[0:256], w_out[1]))
    out[...] = norm_rows(y, last_gain[...]).reshape(16, 16, WIDTH).astype(jnp.bfloat16)


def outer(*arrays):
    scratch = [192, 512, 512, 128, 384, 384, 384]
    return call(
        outer_kernel,
        "outer",
        [(16, 16, WIDTH)],
        [VMEM] * 24,
        scratch=[pltpu.VMEM((rows, WIDTH), jnp.bfloat16) for rows in scratch],
        mib=14,
    )(*arrays)[0]


def swap(x, axis, shift):
    count = lax.axis_size(axis)
    pairs = [(i, ((i + shift) ^ 1) - shift) for i in range(count)]
    if axis == "az":
        pairs = [(i, j % count) for i, j in pairs]
    return lax.ppermute(x, axis, [(i, j) for i, j in pairs if 0 <= j < count])


def per_device(
    hidden_site_vector,
    mesh_portion_descriptors,
    mesh_entry_site,
    mesh_portion_tally,
    incline_grid_position,
    incline_vector_lookup,
    mesh_mapping_matrix,
    prefocus_rescale_factor,
    probe_lock_payload_matrix,
    sharpness_scale,
    final_mapping_matrix,
    terminal_rescale_factor,
):
    packed = pack(
        mesh_portion_descriptors.reshape(128, 8, 2, 128), mesh_entry_site.reshape(16, 128), mesh_portion_tally
    )
    arrived = lax.all_to_all(packed, ("az", "rad"), split_axis=0, concat_axis=0, tiled=True)

    hidden = hidden_site_vector[0]
    block_ones = jnp.asarray(np.kron(np.eye(4), np.ones((64, 64))), jnp.bfloat16)
    pitch, scale, to_a, to_b = stage(
        packed, incline_grid_position, sharpness_scale, incline_vector_lookup, hidden
    )
    hid_a, hid_b = swap(to_a, "rad", 0), swap(to_b, "rad", 1)

    feat, to_a, to_b = cell_sums(arrived)
    feat_a, feat_b = swap(to_a, "rad", 0), swap(to_b, "rad", 1)
    hid, to_a, to_b = widen(feat, hidden, hid_a, hid_b)
    hid_b, hid_a = swap(to_b, "az", 1), swap(to_a, "az", 0)
    stream, to_a, to_b = band(feat, feat_b, feat_a, hid, pitch, mesh_mapping_matrix)
    feat_b, feat_a = swap(to_b, "az", 1), swap(to_a, "az", 0)
    q_aug, k_aug, q_aug_1, k_aug_1 = window_tables()
    weights = (scale, prefocus_rescale_factor, probe_lock_payload_matrix, final_mapping_matrix)
    middle = inner(stream, *weights, block_ones, q_aug, k_aug)
    out = outer(
        feat_b, feat_a, hid_b, hid_a, stream, pitch, mesh_mapping_matrix, *weights, terminal_rescale_factor[None, :],
        block_ones, q_aug, k_aug, q_aug_1, k_aug_1, *middle,
    )
    return out[None]


def solution(mesh):
    rows = P(("az", "rad"), None)
    in_specs = (P(None, "az", "rad", None), rows, P(("az", "rad")), rows) + (P(),) * 8
    return jax.shard_map(
        per_device,
        mesh=mesh,
        in_specs=in_specs,
        out_specs=P(None, "az", "rad", None),
        check_vma=False,
    )
```

```python
import jax
import jax.numpy as jnp
import numpy as np
from jax import lax
from jax.experimental import pallas as pl
from jax.experimental.pallas import tpu as pltpu
from jax.sharding import PartitionSpec as P

HALO = 4
HEADS = 8
WIDTH = 512
EDGE = 2 * HALO
DEAD = 256
NEG = -1024.0
LOG2E = 1.4426950408889634
COLUMN_J = np.array(
    list(range(8, 24)) + list(range(24, 28)) + list(range(4, 8)) + list(range(0, 4)) + list(range(28, 32))
)
SMEM = pl.BlockSpec(memory_space=pltpu.SMEM)
VMEM = pl.BlockSpec(memory_space=pltpu.VMEM)
HBM = pl.BlockSpec(memory_space=pltpu.HBM)


def window_tables():
    i = np.arange(32)
    key = np.zeros((32, 32, 128), np.float32)
    query = np.zeros((24, 24, 128), np.float32)
    for d in range(24):
        key[:, :, d] = np.where(np.abs(COLUMN_J - COLUMN_J[d]) > HALO, NEG, 0.0)[None, :]
        key[:, :, 24 + d] = np.where(np.abs(i - (d + HALO)) > HALO, NEG, 0.0)[:, None]
        query[:, d, d] = 1.0
        query[d, :, 24 + d] = 1.0
    key[:, :, 48] = np.where(COLUMN_J < 8, NEG, 0.0)[None, :]
    key[:, :, 49] = np.where(COLUMN_J >= 24, NEG, 0.0)[None, :]
    tables = (
        query.reshape(576, 128),
        key.reshape(1024, 128),
        query[4:20, :16].reshape(256, 128),
        key[4:28, :24].reshape(576, 128),
    )
    return [jnp.asarray(t, jnp.bfloat16) for t in tables]


def dot(a, b):
    return jnp.dot(a, b, preferred_element_type=jnp.float32)


def rounded(x):
    return x.astype(jnp.bfloat16).astype(jnp.float32)


def norm_rows(x, gain):
    return x * lax.rsqrt(jnp.mean(x * x, -1, keepdims=True) + 1e-05) * gain


def shape_of(x):
    return x if isinstance(x, jax.ShapeDtypeStruct) else jax.ShapeDtypeStruct(x, jnp.bfloat16)


COST = {"pack": 1.5, "stage": 1, "cell_sums": 2, "band": 1, "widen": 1, "inner": 4, "outer": 8}


def call(kernel, name, outs, in_specs, out_specs=None, scratch=(), mib=8):
    return pl.pallas_call(
        kernel,
        out_shape=[shape_of(x) for x in outs],
        in_specs=in_specs,
        out_specs=out_specs or [VMEM] * len(outs),
        scratch_shapes=scratch,
        compiler_params=pltpu.CompilerParams(vmem_limit_bytes=mib << 20),
        name=name,
        cost_estimate=pl.CostEstimate(
            flops=int(COST[name] * 1e9), bytes_accessed=int(COST[name] * 3e6), transcendentals=0
        ),
    )


def interleave(tasks, depth):
    waiting = list(tasks)
    active = []
    while waiting or active:
        if waiting and len(active) < depth:
            active.append(waiting.pop(0))
        for task in list(active):
            if next(task, True):
                active.remove(task)


def one_by_one(*tasks):
    for task in tasks:
        yield from task


def pack_kernel(rows, cells, tally, packed, token, block, cells_here, tally_here, sems, out_sems):
    ids_load = pltpu.make_async_copy(cells, cells_here, sems.at[8])
    tally_load = pltpu.make_async_copy(tally, tally_here, sems.at[9])
    token_store = pltpu.make_async_copy(cells_here.at[0:8], token, sems.at[10])
    ids_load.start()
    tally_load.start()
    loads = [
        pltpu.make_async_copy(rows.at[:, k], block.at[:, :, pl.ds(128 * k, 128)], sems.at[k]) for k in range(8)
    ]
    for load in loads:
        load.start()
    t = lax.broadcasted_iota(jnp.int32, (128, 128), 0)
    lane = lax.broadcasted_iota(jnp.int32, (128, 128), 1)
    mine = t % 8 == lane // 16
    slot = lane % 16
    pick = jnp.where(mine, 1.0, 0.0).astype(jnp.bfloat16)
    r = lax.axis_index("rad")
    order = (lane // 16 == t % 16 // 2) & (lane % 16 == 2 * r + t % 2)
    order = jnp.where(order, 1.0, 0.0).astype(jnp.bfloat16)
    ids_load.wait()
    tally_load.wait()
    token_store.start()
    here = lax.broadcasted_iota(jnp.int32, (16, 128), 1) // 8 == lax.broadcasted_iota(jnp.int32, (16, 128), 0)
    spread = jnp.where(here, tally_here[...].astype(jnp.float32), 0.0).astype(jnp.bfloat16)
    live = slot[:16].astype(jnp.float32) < dot(spread, pick)
    ids = jnp.where(live, cells_here[...].astype(jnp.float32), float(DEAD))
    ids = jnp.broadcast_to(ids[:, None, :], (16, 8, 128)).reshape(128, 128)
    ids = dot(jnp.where(mine, ids, 0.0).astype(jnp.bfloat16), order)
    for load in loads:
        load.wait()
    stores = [pltpu.make_async_copy(block.at[:, :, 0:1024], packed.at[:, :, 0:1024], out_sems.at[0])]
    stores[0].start()
    for at in range(128):
        block[at, :, 1024:1152] = jnp.broadcast_to(ids[at : at + 1], (2, 128)).astype(jnp.bfloat16)
    stores.append(pltpu.make_async_copy(block.at[:, :, 1024:1152], packed.at[:, :, 1024:1152], out_sems.at[1]))
    stores[1].start()
    for store in stores:
        store.wait()
    token_store.wait()


def pack(rows, cells, tally):
    return call(
        pack_kernel,
        "pack",
        [(128, 2, 1152), jax.ShapeDtypeStruct((8, 128), jnp.int32)],
        [HBM] * 3,
        [HBM] * 2,
        [
            pltpu.VMEM((128, 2, 1152), jnp.bfloat16),
            pltpu.VMEM((16, 128), jnp.int32),
            pltpu.VMEM((1, 128), jnp.int32),
            pltpu.SemaphoreType.DMA((11,)),
            pltpu.SemaphoreType.DMA((2,)),
        ],
        mib=60,
    )(rows, cells, tally)


def stage_kernel(token, pitch_at, sharp, lookup, hidden, pitch, scale, send_a, send_b):
    rows = lax.broadcasted_iota(jnp.int32, (64, 1), 0)
    pitch[...] = jnp.sum(
        jnp.where(rows == pitch_at[0], lookup[...].astype(jnp.float32), 0.0), axis=0, keepdims=True
    )
    head = lax.broadcasted_iota(jnp.int32, (1, WIDTH), 1) // 64
    for layer in range(2):
        line = jnp.zeros((1, WIDTH), jnp.float32)
        for h in range(HEADS):
            line = jnp.where(head == h, sharp[layer, h] * LOG2E, line)
        scale[layer : layer + 1] = line
    even = lax.rem(lax.axis_index("rad"), 2) == 0
    low = hidden[:, :EDGE].astype(jnp.float32)
    high = hidden[:, EDGE:].astype(jnp.float32)
    send_a[...] = jnp.where(even, high, low).astype(jnp.bfloat16)
    send_b[...] = jnp.where(even, low, high).astype(jnp.bfloat16)


def stage(*arrays):
    edge = (16, EDGE, WIDTH)
    row = jax.ShapeDtypeStruct((1, WIDTH), jnp.float32)
    two = jax.ShapeDtypeStruct((2, WIDTH), jnp.float32)
    return call(stage_kernel, "stage", [row, two, edge, edge], [HBM, SMEM, SMEM, VMEM, VMEM])(*arrays)


def cell_sum_kernel(block, feat, send_a, send_b):
    cell = lax.broadcasted_iota(jnp.int32, (256, 128), 0).astype(jnp.float32).astype(jnp.bfloat16)
    one, none = jnp.ones((256, 128), jnp.bfloat16), jnp.zeros((256, 128), jnp.bfloat16)
    total = jnp.zeros((256, 128), jnp.float32)
    ids = jnp.sum(block[:, :, 1024:1152].astype(jnp.float32).reshape(16, 8, 2, 128), axis=1)
    for step in range(4):
        picks = []
        rows = []
        for part in range(4 * step, 4 * step + 4):
            wide = jnp.broadcast_to(ids[part, 0:1], (256, 128)).astype(jnp.bfloat16)
            picks.append(jnp.where(wide == cell, one, none))
            rows += [block[8 * part : 8 * part + 8, :, 128 * k : 128 * k + 128].reshape(16, 128) for k in range(8)]
        total = total + dot(jnp.concatenate(picks, axis=1), jnp.concatenate(rows, axis=0))
    total = rounded(total).reshape(16, 16, 128)
    feat[...] = total.astype(jnp.bfloat16)
    even = lax.rem(lax.axis_index("rad"), 2) == 0
    low = total[:, :EDGE]
    high = total[:, EDGE:]
    send_a[...] = jnp.where(even, high, low).astype(jnp.bfloat16)
    send_b[...] = jnp.where(even, low, high).astype(jnp.bfloat16)


def cell_sums(arrived):
    return call(
        cell_sum_kernel,
        "cell_sums",
        [(16, 16, 128), (16, EDGE, 128), (16, EDGE, 128)],
        [VMEM],
    )(arrived)


def widened(own, got_a, got_b):
    even = lax.rem(lax.axis_index("rad"), 2) == 0
    a = got_a[...].astype(jnp.float32)
    b = got_b[...].astype(jnp.float32)
    from_a = (lax.broadcasted_iota(jnp.int32, a.shape, 1) < HALO) == even
    parts = [own[...].astype(jnp.float32), jnp.where(from_a, a, b), jnp.where(from_a, b, a)]
    return jnp.concatenate(parts, axis=1)


def send_halves(x, to_a, to_b):
    even = lax.rem(lax.axis_index("az"), 2) == 0
    to_a[...] = jnp.where(even, x[EDGE:], x[:EDGE]).astype(jnp.bfloat16)
    to_b[...] = jnp.where(even, x[:EDGE], x[EDGE:]).astype(jnp.bfloat16)


def widen_kernel(token, own, got_a, got_b, wide, to_a, to_b):
    x = widened(own, got_a, got_b)
    wide[...] = x.astype(jnp.bfloat16)
    send_halves(x, to_a, to_b)


def widen(*arrays):
    return call(widen_kernel, "widen", [(16, 32, WIDTH)] + [(EDGE, 32, WIDTH)] * 2, [VMEM] * 4)(*arrays)


def streamed(feat, hid, pitch, w_map):
    x = dot(feat.reshape(-1, 128).astype(jnp.bfloat16), w_map[...])
    return rounded(hid.reshape(-1, WIDTH) + x + pitch[...]).reshape(hid.shape)


def band_kernel(feat, feat_b, feat_a, hid, pitch, w_map, stream, to_a, to_b):
    x = widened(feat, feat_a, feat_b)
    send_halves(x, to_a, to_b)
    stream[...] = streamed(x, hid[...].astype(jnp.float32), pitch, w_map).astype(jnp.bfloat16)


def band(*arrays):
    return call(band_kernel, "band", [(16, 32, WIDTH)] + [(EDGE, 32, 128)] * 2, [VMEM] * 6)(*arrays)


def project(w, layer, block, rows, block_ones, target, at, scale=None, plain=False):
    x = dot(rows, w[layer, :, block * 256 : block * 256 + 256])
    lanes = slice(block % 2 * 256, block % 2 * 256 + 256)
    yield
    if not plain:
        x = rounded(x)
        squares = dot((x * x).astype(jnp.bfloat16), block_ones[...])
        yield
        x = x * lax.rsqrt(squares + 1e-06)
    if scale is not None:
        x = x * scale[layer : layer + 1, lanes]
    target[at : at + x.shape[0], lanes] = x.astype(jnp.bfloat16)


def project_all(w, layer, wide, narrow, block_ones, scale, queries, q_at, keys, values, at):
    parts = [project(w, layer, block, wide, block_ones, keys, at) for block in (2, 3)]
    parts += [project(w, layer, block, narrow, block_ones, queries, q_at, scale) for block in (0, 1)]
    return parts + [project(w, layer, block, wide, block_ones, values, at, plain=True) for block in (4, 5)]


def query_lanes(table):
    r = lax.axis_index("rad")
    lane = lax.broadcasted_iota(jnp.int32, (1, 128), 1)
    ends = ((lane == 48) & (r == 0)) | ((lane == 49) & (r == lax.axis_size("rad") - 1))
    return table + jnp.where(ends, 1.0, 0.0).astype(jnp.bfloat16)


def attend(queries, query_aug, keys, key_aug, values, att, att_at=0):
    n = query_aug.shape[0]
    lane = lax.broadcasted_iota(jnp.int32, (1, 128), 1)
    low = jnp.where(lane < 64, 1.0, 0.0).astype(jnp.bfloat16)
    high = jnp.where(lane < 64, 0.0, 1.0).astype(jnp.bfloat16)
    half = lax.broadcasted_iota(jnp.int32, (n, 128), 1) < 64
    one = jnp.ones((key_aug.shape[0], 128), jnp.bfloat16)

    def pair_of_heads(pair):
        lanes = slice(pair * 128, pair * 128 + 128)

        def rows(parts):
            return jnp.concatenate([ref[at : at + count, lanes] for ref, at, count in parts], axis=0)

        q = rows(queries)
        q = jnp.concatenate(
            [jnp.concatenate([q * low, query_aug], axis=1), jnp.concatenate([q * high, query_aug], axis=1)], axis=0
        )
        k = jnp.concatenate([rows(keys), key_aug], axis=1)
        score = lax.dot_general(q, k, (((1,), (1,)), ((), ())), preferred_element_type=jnp.float32)
        yield
        got = dot(jnp.exp2(score).astype(jnp.bfloat16), jnp.concatenate([rows(values), one], axis=1))
        yield
        top = jnp.where(half, got[:n, :128], got[n:, :128])
        total = jnp.where(half, got[:n, 128:], got[n:, 128:])
        att[att_at : att_at + n, lanes] = (top / total).astype(jnp.bfloat16)

    return [pair_of_heads(pair) for pair in range(HEADS // 2)]


def columns(x, at, count, width):
    return x[at : at + count, :width].reshape(count * width, WIDTH)


def inner_kernel(
    band_stream, scale, gains, w_qkv, w_out, block_ones, q_aug, k_aug,
    queries, keys, values, stream, queries_1, keys_1, values_1, att,
):
    x = band_stream[...].astype(jnp.float32)
    normed = norm_rows(x.reshape(512, WIDTH), gains[0:1, :])
    narrow = columns(normed.reshape(16, 32, WIDTH), 0, 16, 24).astype(jnp.bfloat16)
    wide = normed.astype(jnp.bfloat16)
    interleave(project_all(w_qkv, 0, wide, narrow, block_ones, scale, queries, 0, keys, values, 0), 3)
    pairs = attend(
        [(queries, 96, 192)], query_lanes(q_aug[192:384]), [(keys, 0, 512)], k_aug[256:768], [(values, 0, 512)], att
    )
    interleave(pairs, 2)
    x = rounded(columns(x, 4, 8, 24) + dot(att[...], w_out[0]))
    stream[...] = x.astype(jnp.bfloat16)
    normed = norm_rows(x, gains[1:2, :])
    narrow = columns(normed.reshape(8, 24, WIDTH), 0, 8, 16).astype(jnp.bfloat16)
    wide = normed.astype(jnp.bfloat16)
    interleave(project_all(w_qkv, 1, wide, narrow, block_ones, scale, queries_1, 0, keys_1, values_1, 0), 4)


def inner(*arrays):
    outs = [(384, WIDTH), (512, WIDTH), (512, WIDTH), (192, WIDTH), (128, WIDTH), (192, WIDTH), (192, WIDTH)]
    scratch = [pltpu.VMEM((192, WIDTH), jnp.bfloat16)]
    return call(inner_kernel, "inner", outs, [VMEM] * 8, scratch=scratch, mib=14)(*arrays)


def outer_kernel(
    feat_b, feat_a, hid_b, hid_a, band_stream, pitch, w_map, scale, gains, w_qkv, w_out, last_gain, block_ones, q_aug, k_aug, q_aug_1, k_aug_1,
    q_mid, k_mid, v_mid, stream_mid, q1_mid, k1_mid, v1_mid,
    out, q_end, k_end, v_end, q1_end, k1_end, v1_end, att,
):
    even = lax.rem(lax.axis_index("az"), 2) == 0

    def low_high(from_a, from_b):
        a, b = from_a[...], from_b[...]
        return jnp.concatenate([jnp.where(even, b, a), jnp.where(even, a, b)], axis=0)

    x = streamed(low_high(feat_a, feat_b), low_high(hid_a, hid_b).astype(jnp.float32), pitch, w_map)
    normed = norm_rows(x.reshape(512, WIDTH), gains[0:1, :])
    narrow = columns(normed.reshape(16, 32, WIDTH), 4, 8, 24).astype(jnp.bfloat16)
    wide = normed.astype(jnp.bfloat16)
    interleave(project_all(w_qkv, 0, wide, narrow, block_ones, scale, q_end, 0, k_end, v_end, 0), 3)
    pairs = []
    for part in range(2):
        if part == 0:
            q = [(q_end, 0, 96), (q_mid, 0, 96)]
            k, v = [[(end, 0, 256), (mid, 0, 256)] for end, mid in ((k_end, k_mid), (v_end, v_mid))]
        else:
            q = [(q_mid, 288, 96), (q_end, 96, 96)]
            k, v = [[(mid, 256, 256), (end, 256, 256)] for end, mid in ((k_end, k_mid), (v_end, v_mid))]
        q_lanes = query_lanes(q_aug[384 * part : 384 * part + 192])
        pairs += attend(q, q_lanes, k, k_aug[512 * part : 512 * part + 512], v, att, 192 * part)
    interleave(pairs, 2)
    ours = [columns(band_stream[at : at + 4].astype(jnp.float32), 0, 4, 24) for at in (0, 12)]
    before = [columns(x, 4, 4, 24), *ours, columns(x, 8, 4, 24)]
    y = rounded(jnp.concatenate(before, axis=0) + dot(att[...], w_out[0]))
    normed = norm_rows(y, gains[1:2, :])
    kept = columns(y.reshape(16, 24, WIDTH), 4, 8, 16)
    narrow = columns(normed.reshape(16, 24, WIDTH), 4, 8, 16).astype(jnp.bfloat16)
    wide = normed.astype(jnp.bfloat16)
    interleave(project_all(w_qkv, 1, wide, narrow, block_ones, scale, q1_end, 0, k1_end, v1_end, 0), 4)
    pairs = []
    for part in range(2):
        if part == 0:
            q = [(q1_end, 0, 64), (q1_mid, 0, 64)]
            k, v = [[(end, 0, 192), (mid, 0, 192)] for end, mid in ((k1_end, k1_mid), (v1_end, v1_mid))]
        else:
            q = [(q1_mid, 64, 64), (q1_end, 64, 64)]
            k, v = [[(mid, 0, 192), (end, 192, 192)] for end, mid in ((k1_end, k1_mid), (v1_end, v1_mid))]
        q_lanes = query_lanes(q_aug_1[128 * part : 128 * part + 128])
        pairs += attend(q, q_lanes, k, k_aug_1[192 * part : 192 * part + 384], v, att, 128 * part)
    interleave(pairs, 2)
    middle = columns(stream_mid[...].astype(jnp.float32).reshape(8, 24, WIDTH), 0, 8, 16)
    before = jnp.concatenate([kept[:64], middle, kept[64:]], axis=0)
    y = rounded(before + dot(att[0:256], w_out[1]))
    out[...] = norm_rows(y, last_gain[...]).reshape(16, 16, WIDTH).astype(jnp.bfloat16)


def outer(*arrays):
    scratch = [192, 512, 512, 128, 384, 384, 384]
    return call(
        outer_kernel,
        "outer",
        [(16, 16, WIDTH)],
        [VMEM] * 24,
        scratch=[pltpu.VMEM((rows, WIDTH), jnp.bfloat16) for rows in scratch],
        mib=14,
    )(*arrays)[0]


def swap(x, axis, shift):
    count = lax.axis_size(axis)
    pairs = [(i, ((i + shift) ^ 1) - shift) for i in range(count)]
    if axis == "az":
        pairs = [(i, j % count) for i, j in pairs]
    return lax.ppermute(x, axis, [(i, j) for i, j in pairs if 0 <= j < count])


def per_device(
    hidden_site_vector,
    mesh_portion_descriptors,
    mesh_entry_site,
    mesh_portion_tally,
    incline_grid_position,
    incline_vector_lookup,
    mesh_mapping_matrix,
    prefocus_rescale_factor,
    probe_lock_payload_matrix,
    sharpness_scale,
    final_mapping_matrix,
    terminal_rescale_factor,
):
    packed, token = pack(
        mesh_portion_descriptors.reshape(128, 8, 2, 128), mesh_entry_site.reshape(16, 128), mesh_portion_tally
    )
    arrived = lax.all_to_all(packed, ("az", "rad"), split_axis=0, concat_axis=0, tiled=True)

    hidden = hidden_site_vector[0]
    block_ones = jnp.asarray(np.kron(np.eye(4), np.ones((64, 64))), jnp.bfloat16)
    pitch, scale, to_a, to_b = stage(
        token, incline_grid_position, sharpness_scale, incline_vector_lookup, hidden
    )
    hid_a, hid_b = swap(to_a, "rad", 0), swap(to_b, "rad", 1)

    feat, to_a, to_b = cell_sums(arrived)
    feat_a, feat_b = swap(to_a, "rad", 0), swap(to_b, "rad", 1)
    hid, to_a, to_b = widen(feat, hidden, hid_a, hid_b)
    hid_b, hid_a = swap(to_b, "az", 1), swap(to_a, "az", 0)
    stream, to_a, to_b = band(feat, feat_b, feat_a, hid, pitch, mesh_mapping_matrix)
    feat_b, feat_a = swap(to_b, "az", 1), swap(to_a, "az", 0)
    q_aug, k_aug, q_aug_1, k_aug_1 = window_tables()
    weights = (scale, prefocus_rescale_factor, probe_lock_payload_matrix, final_mapping_matrix)
    middle = inner(stream, *weights, block_ones, q_aug, k_aug)
    out = outer(
        feat_b, feat_a, hid_b, hid_a, stream, pitch, mesh_mapping_matrix, *weights, terminal_rescale_factor[None, :],
        block_ones, q_aug, k_aug, q_aug_1, k_aug_1, *middle,
    )
    return out[None]


def solution(mesh):
    rows = P(("az", "rad"), None)
    in_specs = (P(None, "az", "rad", None), rows, P(("az", "rad")), rows) + (P(),) * 8
    return jax.shard_map(
        per_device,
        mesh=mesh,
        in_specs=in_specs,
        out_specs=P(None, "az", "rad", None),
        check_vma=False,
    )
```
